32 devices in a mesh: batch: 4 (over z), space: 8 (over y, x, core).
Axes of the slice: x: 2, y: 2, z: 4, core: 2. Of those that a mesh axis runs over, the one named last changes fastest.
Arguments:
- density: bfloat16 [8, 4, 16, 16, 256], P('batch', None, 'space'), may hold values from -6 to 6
- w_first: bfloat16 [32, 108], replicated, may hold values from -0.625 to 0.625
- b_first: float32 [32], replicated, may hold values from -3 to 3
- w_second: bfloat16 [64, 864], replicated, may hold values from -0.4375 to 0.4375
- b_second: float32 [64], replicated, may hold values from -3 to 3
- cotangent: bfloat16 [8, 64, 8, 8, 128], P('batch', None, 'space'), may hold values from -6 to 6
Outputs:
- features: bfloat16 [8, 64, 8, 8, 128], P('batch', None, 'space')
- grad_w_first: float32 [32, 108], replicated
- grad_b_first: float32 [32], replicated
- grad_w_second: float32 [64, 864], replicated
- grad_b_second: float32 [64], replicated
The draws below stay inside these ranges and needn't reach their ends.
All inputs are finite; a program needn't handle non-finite values.
Results may differ from the reference program's by a relative error of at most 0.0095.
Values may be sent and summed in bfloat16 or wider, within the bound.
A program may use at most 128 MiB of HBM per device.

```python
import jax
import jax.numpy as jnp
from jax import lax

C0 = 4
C1 = 32
C2 = 64
TAPS = 27
X = 16
Y = 256
CUBES = 8
NZ = 16


def block_scale(stream_key, dims, shards, low, top_value):
    gain, own = 1.0, jax.random.fold_in(stream_key, 6)
    for position, blocks in shards:
        steps = jnp.exp(jax.random.uniform(jax.random.fold_in(own, position), (blocks,), jnp.float32, low / len(shards), top_value / len(shards)))
        gain = gain * jnp.repeat(steps, dims[position] // blocks).reshape([-1 if axis == position else 1 for axis in range(len(dims))])
    return gain


def normal_values(own_key, shape, scale, reach, split=(), held_as=jnp.bfloat16):
    entries = scale * jax.random.normal(own_key, shape, jnp.float32)
    if split:
        entries = entries * block_scale(own_key, shape, split, -0.22, 0.18)
    return jnp.clip(entries, -reach, reach).astype(held_as)


def setup_inputs(seed: int = 0) -> dict:
    key_of = jax.random.split(jax.random.key(seed), 7)
    return {
        "density": normal_values(key_of[0], (CUBES, C0, NZ, X, Y), 1.0, 6.0, ((0, 4), (2, 8))),
        "w_first": normal_values(key_of[1], (C1, TAPS * C0), (TAPS * C0) ** -0.5, 0.625),
        "b_first": normal_values(key_of[2], (C1,), 0.5, 3.0, (), jnp.float32),
        "w_second": normal_values(key_of[3], (C2, TAPS * C1), (TAPS * C1 // 4) ** -0.5, 0.4375),
        "b_second": normal_values(key_of[4], (C2,), 0.5, 3.0, (), jnp.float32),
        "cotangent": normal_values(key_of[5], (CUBES, C2, NZ // 2, X // 2, Y // 2), 1.0, 6.0, ((0, 4), (2, 8))),
    }


def patches(padded, planes, height, length):
    pieces = []
    for i in range(3):
        for j in range(3):
            for k in range(3):
                pieces.append(padded[:, i:i + planes, j:j + height, k:k + length])
    stacked = jnp.stack(pieces, axis=0)
    return stacked.reshape((-1, planes, height, length))


def pad_all(field):
    return jnp.pad(field, ((0, 0), (1, 1), (1, 1), (1, 1)))


def dsilu(value):
    sig = jax.nn.sigmoid(value)
    return sig * (1.0 + value * (1.0 - sig))


def pool(field):
    chans, planes, height, length = field.shape
    return field.reshape(chans, planes // 2, 2, height // 2, 2, length // 2, 2).mean(axis=(2, 4, 6))


def spread(field):
    chans, planes, height, length = field.shape
    big = jnp.broadcast_to(field[:, :, None, :, None, :, None], (chans, planes, 2, height, 2, length, 2))
    return big.reshape(chans, planes * 2, height * 2, length * 2) * 0.125


def flip_taps(weight, inner):
    outer = weight.shape[0]
    return weight.reshape(outer, 27, inner)[:, ::-1, :].transpose(1, 0, 2).reshape(27 * outer, inner)


def one_cube(density, cotangent, w_first, b_first, w_second, b_second):
    chans, planes, height, length = density.shape
    cols_first = patches(pad_all(density), planes, height, length)
    pre_first = jnp.einsum("ok,kzxy->ozxy", w_first.astype(jnp.float32), cols_first.astype(jnp.float32)) + b_first[:, None, None, None]
    pooled = pool(jax.nn.silu(pre_first)).astype(jnp.bfloat16)
    cols_second = patches(pad_all(pooled), planes // 2, height // 2, length // 2)
    pre_second = jnp.einsum("ok,kzxy->ozxy", w_second.astype(jnp.float32), cols_second.astype(jnp.float32)) + b_second[:, None, None, None]
    features = jax.nn.silu(pre_second).astype(jnp.bfloat16)
    grad_second = (cotangent.astype(jnp.float32) * dsilu(pre_second)).astype(jnp.bfloat16)
    gw_second = jnp.einsum("ozxy,kzxy->ok", grad_second.astype(jnp.float32), cols_second.astype(jnp.float32))
    gb_second = jnp.sum(grad_second.astype(jnp.float32), axis=(1, 2, 3))
    flipped = flip_taps(w_second, w_second.shape[1] // 27)
    cols_back = patches(pad_all(grad_second), planes // 2, height // 2, length // 2)
    back = jnp.einsum("kc,kzxy->czxy", flipped.astype(jnp.float32), cols_back.astype(jnp.float32))
    grad_first = (spread(back) * dsilu(pre_first)).astype(jnp.bfloat16)
    gw_first = jnp.einsum("ozxy,kzxy->ok", grad_first.astype(jnp.float32), cols_first.astype(jnp.float32))
    gb_first = jnp.sum(grad_first.astype(jnp.float32), axis=(1, 2, 3))
    return features, gw_first, gb_first, gw_second, gb_second


def reference(density, w_first, b_first, w_second, b_second, cotangent):
    def apply_cube(pair):
        return one_cube(pair[0], pair[1], w_first, b_first, w_second, b_second)

    features, gw_first, gb_first, gw_second, gb_second = lax.map(apply_cube, (density, cotangent))
    return features, jnp.sum(gw_first, axis=0), jnp.sum(gb_first, axis=0), jnp.sum(gw_second, axis=0), jnp.sum(gb_second, axis=0)
```

```python
import functools

import jax
import jax.numpy as jnp
import numpy as np
from jax import lax
from jax.experimental import pallas as pl
from jax.experimental.pallas import tpu as pltpu
from jax.sharding import PartitionSpec as P

F32 = jnp.float32
BF16 = jnp.bfloat16
MESH = pl.DeviceIdType.MESH
NT = (((1,), (1,)), ((), ()))


def fold_matrix():
    fold = np.zeros((128, 8, 256), np.float32)

    def coordinate(group, parity):
        return 1 + parity if group == 0 else (0 if parity == 1 else 3)

    planes = (1, 2, 0, 3)
    for row in range(256):
        zi, xg, yg = row >> 6, (row >> 5) & 1, (row >> 4) & 1
        yp, xp, c = (row >> 3) & 1, (row >> 2) & 1, row & 3
        zz, xx, yy = planes[zi], coordinate(xg, xp), coordinate(yg, yp)
        for pos in range(8):
            i, j, k = zz - (pos >> 2), xx - ((pos >> 1) & 1), yy - (pos & 1)
            if 0 <= i < 3 and 0 <= j < 3 and 0 <= k < 3:
                fold[((i * 3 + j) * 3 + k) * 4 + c, pos, row] = 1
    return fold.reshape(128, 2048)


def iota(shape, axis):
    return lax.broadcasted_iota(jnp.int32, shape, axis)


def sigmoid(value):
    return 0.5 + 0.5 * jnp.tanh(0.5 * value)


def column_of(row):
    size = row.shape[1]
    eye = iota((size, size), 0) == iota((size, size), 1)
    return jnp.sum(jnp.where(eye, row, 0.0), axis=1, keepdims=True)


def row_of(column):
    size = column.shape[0]
    eye = iota((size, size), 0) == iota((size, size), 1)
    return jnp.sum(jnp.where(eye, column, 0.0), axis=0, keepdims=True)


def dot(a, b):
    return jnp.dot(a, b, preferred_element_type=F32)


def dot_nt(a, b):
    return lax.dot_general(a, b, NT, preferred_element_type=F32)


def before(tile):
    axis = tile.ndim - 1
    return jnp.where(iota(tile.shape, axis) == 0, 0.0, pltpu.roll(tile, 1, axis))


def after(tile):
    axis = tile.ndim - 1
    return jnp.where(iota(tile.shape, axis) == 127, 0.0, pltpu.roll(tile, 127, axis))


def kernel(
    nb, ns,
    dens, w1_hbm, b1_hbm, w2_hbm, b2_hbm, cot_hbm, fold_hbm,
    feat, gw1_out, gb1_out, gw2_out, gb2_out,
    w1, b1, w2, b2, cot, fold, buf, cols1, wbig, d1, w1s, w2s, w2c, wb, pooled, halo2, c9, acc2, trans, gs, cb, bsend, brecv, bown, gf,
    part, rs_recv, mine, bx_recv, full, small, sm_recv, sm_mid, sm_recv2,
    load_sem, in_sem, dsend, drecv, psend, precv, ksend, krecv, rsend, rrecv, xsend, xrecv, gsend, grecv,
    s1send, s1recv, s2send, s2recv,
):
    bi = lax.axis_index("batch")
    si = lax.axis_index("space")
    has_prev, has_next = si > 0, si < ns - 1
    prev, nxt = (bi, jnp.maximum(si - 1, 0)), (bi, jnp.minimum(si + 1, ns - 1))

    def space_peer(d):
        return (bi, lax.rem(si + d, ns))

    def batch_peer(d):
        return (lax.rem(bi + d, nb), si)

    barrier = pltpu.get_barrier_semaphore()

    def hello_space(d, carry):
        pl.semaphore_signal(barrier, inc=1, device_id=space_peer(d), device_id_type=MESH)
        return carry

    def hello_batch(d, carry):
        pl.semaphore_signal(barrier, inc=1, device_id=batch_peer(d), device_id_type=MESH)
        return carry

    lax.fori_loop(1, ns, hello_space, 0)
    lax.fori_loop(1, nb, hello_batch, 0)
    loads = [pltpu.make_async_copy(dens.at[:, :, z], buf.at[z], load_sem.at[z]) for z in range(2)]
    pairs = ((w1_hbm, w1), (fold_hbm, fold), (w2_hbm, w2), (b1_hbm, b1), (b2_hbm, b2), (cot_hbm, cot))
    params = [pltpu.make_async_copy(src, dst, in_sem.at[n]) for n, (src, dst) in enumerate(pairs)]
    for copy in loads + params:
        copy.start()
    pl.semaphore_wait(barrier, ns - 1 + nb - 1)

    def remote(src, dst, send, recv, target):
        return pltpu.make_async_remote_copy(
            src_ref=src, dst_ref=dst, send_sem=send, recv_sem=recv, device_id=target, device_id_type=MESH
        )

    dens_copies = [
        remote(dens.at[:, :, 1], buf.at[2], dsend.at[0], drecv.at[0], nxt),
        remote(dens.at[:, :, 0], buf.at[3], dsend.at[1], drecv.at[1], prev),
    ]
    pool_copies = [
        [
            remote(pooled.at[b], halo2.at[b, side], psend.at[b, side], precv.at[b, side], (nxt, prev)[side])
            for side in range(2)
        ]
        for b in range(2)
    ]
    back_copies = [
        [
            remote(bsend.at[b, side], brecv.at[b, side], ksend.at[b, side], krecv.at[b, side], (nxt, prev)[side])
            for side in range(2)
        ]
        for b in range(2)
    ]
    gives, takes = (has_next, has_prev), (has_prev, has_next)

    def start(copies):
        for side in range(2):
            pl.when(gives[side])(copies[side].start)

    def wait_in(copies):
        for side in range(2):
            pl.when(takes[side])(copies[side].wait_recv)

    def wait_out(copies):
        for side in range(2):
            pl.when(gives[side])(copies[side].wait_send)

    start(dens_copies)

    for side in range(2):
        def clear(side=side):
            buf[2 + side] = jnp.zeros(buf.shape[1:], BF16)
            for b in range(2):
                halo2[b, side] = jnp.zeros(halo2.shape[2:], BF16)
                brecv[b, side] = jnp.zeros(brecv.shape[2:], BF16)
        pl.when(jnp.logical_not(takes[side]))(clear)

    for copy in params:
        copy.wait()
    w1s[...] = jnp.zeros(w1s.shape, F32)
    w1s[:, 0:108] = w1[...].astype(F32)
    w1v = w1s[...].astype(BF16)
    for pos in range(8):
        wbig[pos * 32:(pos + 1) * 32, :] = dot(w1v, fold[:, pos * 256:(pos + 1) * 256]).astype(BF16)
    w2s[...] = jnp.zeros(w2s.shape, F32)
    w2s[:, 0:864] = w2[...].astype(F32)
    planes = (1, 0, 2)
    for j in range(3):
        for slot, i in enumerate(planes):
            lane = i * 288 + j * 96
            w2c[j * 64:(j + 1) * 64, slot * 96:(slot + 1) * 96] = w2s[:, lane:lane + 96].astype(BF16)
    for t4 in range(7):
        turned = w2s[:, t4 * 128:(t4 + 1) * 128].T
        for quarter in range(4):
            t = t4 * 4 + quarter
            if t < 27:
                i, j, k = t // 9, (t // 3) % 3, t % 3
                block = turned[quarter * 32:(quarter + 1) * 32, :]
                wb[j * 96 + i * 32:j * 96 + (i + 1) * 32, k * 64:(k + 1) * 64] = block.astype(BF16)
    bias1 = column_of(b1[...])
    bias1 = jnp.concatenate([bias1] * 8, axis=0)
    bias2 = column_of(b2[...])
    c9[...] = jnp.zeros(c9.shape, BF16)
    cb[...] = jnp.zeros(cb.shape, BF16)
    part[448:512, :] = jnp.zeros((64, 128), BF16)

    r, s = iota((256, 256), 0), iota((256, 256), 1)
    rows = (r & 192) + (r & 3) * 16 + ((r >> 3) & 7) * 2 + ((r >> 2) & 1)
    move_rows = (rows == s).astype(F32).astype(BF16)
    move_lanes = (r == (s & 127) * 2 + (s >> 7)).astype(F32).astype(BF16)

    def lay_out(pair):
        flat = buf[pair * 2:pair * 2 + 2].reshape(256, 256)
        moved = dot(move_rows, dot(flat, move_lanes).astype(BF16)).reshape(4, 8, 8, 256)
        gap = jnp.zeros((4, 1, 8, 256), F32)
        low = jnp.concatenate([gap, moved[:, :7]], axis=1)
        high = jnp.concatenate([moved[:, 1:], gap], axis=1)
        odd = iota(moved.shape, 2) >= 4
        beside = jnp.where(odd, low, high)
        for xg, field in enumerate((moved, beside)):
            even_y, odd_y = field[..., :128], field[..., 128:]
            for yg in range(2):
                halves = (even_y, odd_y) if yg == 0 else (after(even_y), before(odd_y))
                tile = jnp.concatenate(halves, axis=2).astype(BF16)
                for z in range(2):
                    row = ((pair * 2 + z) * 4 + xg * 2 + yg) * 16
                    for b in range(2):
                        for x in range(8):
                            lane = (b * 8 + x) * 128
                            cols1[row:row + 16, lane:lane + 128] = tile[z * 2 + b, x]

    for copy in loads:
        copy.wait()
    lay_out(0)
    wait_in(dens_copies)
    lay_out(1)

    def fill(target, row, height, b, field, flip):
        for x in range(8):
            lane = (b * 10 + 1 + x) * 128
            tile = field[:, x * 128:(x + 1) * 128]
            shifts = (before(tile), tile, after(tile))
            for k in range(3):
                piece = shifts[2 - k] if flip else shifts[k]
                target[row + k * height:row + (k + 1) * height, lane:lane + 128] = piece.astype(BF16)

    for b in range(2):
        for q in range(4):
            lane = b * 1024 + q * 256
            pre = dot(wbig[...], cols1[:, lane:lane + 256]) + bias1
            sig = sigmoid(pre)
            act = pre * sig
            d1[:, lane:lane + 256] = sig + act - act * sig
            total = act[0:32]
            for pos in range(1, 8):
                total = total + act[pos * 32:(pos + 1) * 32]
            pooled[b, :, q * 256:(q + 1) * 256] = (total * 0.125).astype(BF16)
        start(pool_copies[b])
    for b in range(2):
        fill(c9, 0, 32, b, pooled[b].astype(F32), False)
        acc2[b] = dot(w2c[:, 0:96], c9[0:96, b * 1280:(b + 1) * 1280])
        trans[b] = cot[b].astype(F32)

    gb2 = jnp.zeros((64, 1), F32)
    for b in range(2):
        wait_in(pool_copies[b])
        for side in range(2):
            fill(c9, 96 + side * 96, 32, b, halo2[b, side].astype(F32), False)
        acc = acc2[b] + dot(w2c[:, 96:288], c9[96:288, b * 1280:(b + 1) * 1280])
        pre = acc[0:64, 0:1024] + acc[64:128, 128:1152] + acc[128:192, 256:1280] + bias2
        sig = sigmoid(pre)
        act = pre * sig
        slope = sig + act - act * sig
        grads = []
        for x in range(8):
            grads.append(trans[b, pl.ds(x, 64, stride=8), :] * slope[:, x * 128:(x + 1) * 128])
        grad = jnp.concatenate(grads, axis=1).astype(BF16)
        gs[:, b * 1024:(b + 1) * 1024] = grad
        grad = grad.astype(F32)
        gb2 = gb2 + jnp.sum(grad, axis=1, keepdims=True)
        fill(cb, 0, 64, b, grad, True)
        acc = dot(wb[...], cb[:, b * 1280:(b + 1) * 1280])
        give = acc[0:96, 256:1280] + acc[96:192, 128:1152] + acc[192:288, 0:1024]
        bsend[b, 1] = give[0:32].astype(BF16)
        bsend[b, 0] = give[64:96].astype(BF16)
        start(back_copies[b])
        bown[:, b * 1024:(b + 1) * 1024] = give[32:64]
        for x in range(8):
            trans[b, pl.ds(x, 64, stride=8), :] = act[:, x * 128:(x + 1) * 128]
        feat[b] = trans[b].astype(BF16)

    for j in range(3):
        total = None
        for b in range(2):
            lane = b * 1280 + j * 128
            term = dot_nt(gs[:, b * 1024:(b + 1) * 1024], c9[:, lane:lane + 1024])
            total = term if total is None else total + term
        for slot, i in enumerate(planes):
            lane = i * 288 + j * 96
            w2s[:, lane:lane + 96] = total[:, slot * 96:(slot + 1) * 96]
    for t in range(7):
        part[t * 64:(t + 1) * 64, :] = w2s[:, t * 128:(t + 1) * 128].astype(BF16)

    size = 512 // ns

    def chunk(index):
        return pl.ds(pl.multiple_of(index * size, size), size)

    def rs_copy(d):
        return remote(part.at[chunk(lax.rem(si + d, ns))], rs_recv.at[d], rsend.at[d], rrecv.at[d], space_peer(d))

    def bx_copy(d):
        return remote(mine.at[0], bx_recv.at[bi], xsend.at[d], xrecv.at[d], batch_peer(d))

    def ag_copy(d):
        return remote(mine.at[1], full.at[chunk(si)], gsend.at[d], grecv.at[d], space_peer(d))

    def s1_copy(d):
        return remote(small, sm_recv.at[si], s1send.at[d], s1recv.at[d], space_peer(d))

    def s2_copy(d):
        return remote(sm_mid, sm_recv2.at[bi], s2send.at[d], s2recv.at[d], batch_peer(d))

    def each(count, make, act):
        def step(d, carry):
            act(make(d))
            return carry
        lax.fori_loop(1, count, step, 0)

    def go(copy):
        copy.start()

    def arrive(copy):
        copy.wait_recv()

    def leave(copy):
        copy.wait_send()

    def in_order(terms, count):
        total = terms[0].astype(F32)
        for index in range(1, count):
            total = total + terms[index].astype(F32)
        return total

    each(ns, rs_copy, go)

    gb1 = jnp.zeros((32, 256), F32)
    for b in range(2):
        wait_in(back_copies[b])
        for q in range(4):
            lane = b * 1024 + q * 256
            near = brecv[b, :, :, q * 256:(q + 1) * 256].astype(F32)
            back = (bown[:, lane:lane + 256] + near[0] + near[1]) * 0.125
            for pos in range(8):
                piece = (back * d1[pos * 32:(pos + 1) * 32, lane:lane + 256]).astype(BF16)
                gf[pos * 32:(pos + 1) * 32, lane:lane + 256] = piece
                gb1 = gb1 + piece.astype(F32)
    gram = dot_nt(gf[...], cols1[...])
    high = gram.astype(BF16)
    low = (gram - high.astype(F32)).astype(BF16)
    folded = jnp.zeros((64, 128), F32)
    for pos in range(8):
        both = jnp.concatenate([high[pos * 32:(pos + 1) * 32], low[pos * 32:(pos + 1) * 32]], axis=0)
        folded = folded + dot_nt(both, fold[:, pos * 256:(pos + 1) * 256])
    lane = iota((32, 128), 1)
    sums = folded[0:32] + folded[32:64]
    sums = jnp.where(lane == 108, jnp.sum(gb1, axis=1, keepdims=True), sums)
    sums = jnp.where(lane == 109, gb2[0:32], sums)
    small[...] = jnp.where(lane == 110, gb2[32:64], sums).astype(BF16)
    each(ns, s1_copy, go)

    each(ns, rs_copy, arrive)
    total = part[chunk(si), :].astype(F32)
    for d in range(1, ns):
        total = total + rs_recv[d].astype(F32)
    total = total.astype(BF16)
    mine[0] = total
    bx_recv[bi] = total
    each(nb, bx_copy, go)

    each(ns, s1_copy, arrive)
    sm_recv[si] = small[...]
    total = in_order(sm_recv, ns).astype(BF16)
    sm_mid[...] = total
    sm_recv2[bi] = total
    each(nb, s2_copy, go)

    each(nb, bx_copy, arrive)
    total = in_order(bx_recv, nb).astype(BF16)
    mine[1] = total
    full[chunk(si), :] = total
    each(ns, ag_copy, go)

    each(nb, s2_copy, arrive)
    total = in_order(sm_recv2, nb)
    gw1_out[...] = total[:, 0:108]
    gb1_out[...] = row_of(total[:, 108:109])
    gb2_out[...] = row_of(jnp.concatenate([total[:, 109:110], total[:, 110:111]], axis=0))

    each(ns, ag_copy, arrive)
    for t in range(7):
        width = min(128, 864 - t * 128)
        gw2_out[:, t * 128:t * 128 + width] = full[t * 64:(t + 1) * 64, 0:width].astype(F32)

    wait_out(dens_copies)
    for b in range(2):
        wait_out(pool_copies[b])
        wait_out(back_copies[b])
    each(ns, rs_copy, leave)
    each(nb, bx_copy, leave)
    each(ns, ag_copy, leave)
    each(ns, s1_copy, leave)
    each(nb, s2_copy, leave)


def hand_out(*refs):
    held, results, sems = refs[0:5], refs[5:10], refs[10]
    outward = [pltpu.make_async_copy(held[n], results[n], sems.at[n]) for n in range(5)]
    for copy in outward:
        copy.start()
    for copy in outward:
        copy.wait()


def body(nb, ns, density, w_first, b_first, w_second, b_second, cotangent):
    vmem = pl.BlockSpec(memory_space=pltpu.VMEM)
    hbm = pl.BlockSpec(memory_space=pltpu.HBM)
    dma = pltpu.SemaphoreType.DMA
    size = 512 // ns
    shapes = (
        jax.ShapeDtypeStruct((2, 512, 128), BF16),
        jax.ShapeDtypeStruct((32, 108), F32),
        jax.ShapeDtypeStruct((1, 32), F32),
        jax.ShapeDtypeStruct((64, 864), F32),
        jax.ShapeDtypeStruct((1, 64), F32),
    )
    held = pl.pallas_call(
        functools.partial(kernel, nb, ns),
        out_shape=tuple(pltpu.VMEM(one.shape, one.dtype) for one in shapes),
        in_specs=[hbm] * 7,
        out_specs=(vmem,) * 5,
        scratch_shapes=[
            pltpu.VMEM((32, 108), BF16),
            pltpu.VMEM((1, 32), F32),
            pltpu.VMEM((64, 864), BF16),
            pltpu.VMEM((1, 64), F32),
            pltpu.VMEM((2, 512, 128), BF16),
            pltpu.VMEM((128, 2048), BF16),
            pltpu.VMEM((4, 2, 4, 16, 256), BF16),
            pltpu.VMEM((256, 2048), BF16),
            pltpu.VMEM((256, 256), BF16),
            pltpu.VMEM((256, 2048), F32),
            pltpu.VMEM((32, 128), F32),
            pltpu.VMEM((64, 896), F32),
            pltpu.VMEM((192, 288), BF16),
            pltpu.VMEM((288, 192), BF16),
            pltpu.VMEM((2, 32, 1024), BF16),
            pltpu.VMEM((2, 2, 32, 1024), BF16),
            pltpu.VMEM((288, 2560), BF16),
            pltpu.VMEM((2, 192, 1280), F32),
            pltpu.VMEM((2, 512, 128), F32),
            pltpu.VMEM((64, 2048), BF16),
            pltpu.VMEM((192, 2560), BF16),
            pltpu.VMEM((2, 2, 32, 1024), BF16),
            pltpu.VMEM((2, 2, 32, 1024), BF16),
            pltpu.VMEM((32, 2048), F32),
            pltpu.VMEM((256, 2048), BF16),
            pltpu.VMEM((512, 128), BF16),
            pltpu.VMEM((ns, size, 128), BF16),
            pltpu.VMEM((2, size, 128), BF16),
            pltpu.VMEM((nb, size, 128), BF16),
            pltpu.VMEM((512, 128), BF16),
            pltpu.VMEM((32, 128), BF16),
            pltpu.VMEM((ns, 32, 128), BF16),
            pltpu.VMEM((32, 128), BF16),
            pltpu.VMEM((nb, 32, 128), BF16),
            dma((2,)), dma((6,)), dma((2,)), dma((2,)),
            dma((2, 2)), dma((2, 2)), dma((2, 2)), dma((2, 2)),
            dma((ns,)), dma((ns,)), dma((nb,)), dma((nb,)), dma((ns,)), dma((ns,)),
            dma((ns,)), dma((ns,)), dma((nb,)), dma((nb,)),
        ],
        compiler_params=pltpu.CompilerParams(
            collective_id=0, has_side_effects=True, vmem_limit_bytes=40 * 1024 * 1024
        ),
        cost_estimate=pl.CostEstimate(flops=1 << 30, bytes_accessed=1 << 21, transcendentals=1 << 20),
    )(*[
        pltpu.with_memory_space_constraint(one, pltpu.HBM)
        for one in (
            density, w_first, b_first.reshape(1, 32), w_second, b_second.reshape(1, 64), cotangent.reshape(2, 512, 128),
            jnp.asarray(fold_matrix(), BF16),
        )
    ])
    feat, gw1, gb1, gw2, gb2 = pl.pallas_call(
        hand_out,
        out_shape=shapes,
        in_specs=[vmem] * 5,
        out_specs=(hbm,) * 5,
        scratch_shapes=[dma((5,))],
        compiler_params=pltpu.CompilerParams(vmem_limit_bytes=8 * 1024 * 1024),
    )(*held)
    return feat.reshape(cotangent.shape), gw1, gb1.reshape(32), gw2, gb2.reshape(64)


def solution(mesh):
    data = P("batch", None, "space", None, None)
    return jax.shard_map(
        functools.partial(body, mesh.shape["batch"], mesh.shape["space"]),
        mesh=mesh,
        in_specs=(data, P(), P(), P(), P(), data),
        out_specs=(data, P(), P(), P(), P()),
        check_vma=False,
    )
```

```python
import functools

import jax
import jax.numpy as jnp
import numpy as np
from jax import lax
from jax.experimental import pallas as pl
from jax.experimental.pallas import tpu as pltpu
from jax.sharding import PartitionSpec as P

F32 = jnp.float32
BF16 = jnp.bfloat16
MESH = pl.DeviceIdType.MESH
NT = (((1,), (1,)), ((), ()))


def fold_matrix():
    fold = np.zeros((128, 8, 256), np.float32)

    def coordinate(group, parity):
        return 1 + parity if group == 0 else (0 if parity == 1 else 3)

    planes = (1, 2, 0, 3)
    for row in range(256):
        zi, xg, yg = row >> 6, (row >> 5) & 1, (row >> 4) & 1
        yp, xp, c = (row >> 3) & 1, (row >> 2) & 1, row & 3
        zz, xx, yy = planes[zi], coordinate(xg, xp), coordinate(yg, yp)
        for pos in range(8):
            i, j, k = zz - (pos >> 2), xx - ((pos >> 1) & 1), yy - (pos & 1)
            if 0 <= i < 3 and 0 <= j < 3 and 0 <= k < 3:
                fold[((i * 3 + j) * 3 + k) * 4 + c, pos, row] = 1
    return fold.reshape(128, 2048)


def iota(shape, axis):
    return lax.broadcasted_iota(jnp.int32, shape, axis)


def sigmoid(value):
    return 0.5 + 0.5 * jnp.tanh(0.5 * value)


def column_of(row):
    size = row.shape[1]
    eye = iota((size, size), 0) == iota((size, size), 1)
    return jnp.sum(jnp.where(eye, row, 0.0), axis=1, keepdims=True)


def row_of(column):
    size = column.shape[0]
    eye = iota((size, size), 0) == iota((size, size), 1)
    return jnp.sum(jnp.where(eye, column, 0.0), axis=0, keepdims=True)


def dot(a, b):
    return jnp.dot(a, b, preferred_element_type=F32)


def dot_nt(a, b):
    return lax.dot_general(a, b, NT, preferred_element_type=F32)


def before(tile):
    axis = tile.ndim - 1
    return jnp.where(iota(tile.shape, axis) == 0, 0.0, pltpu.roll(tile, 1, axis))


def after(tile):
    axis = tile.ndim - 1
    return jnp.where(iota(tile.shape, axis) == 127, 0.0, pltpu.roll(tile, 127, axis))


def kernel(
    nb, ns,
    dens, w1_hbm, b1_hbm, w2_hbm, b2_hbm, cot_hbm, fold_hbm,
    feat, gw1_out, gb1_out, gw2_out, gb2_out,
    w1, b1, w2, b2, cot, fold, buf, cols1, wbig, d1, w1s, w2s, w2c, wb, pooled, halo2, c9, acc2, trans, acts, held, gs, cb, bsend, brecv, bown, gf,
    part, rs_recv, mine, bx_recv, full, small, sm_recv, sm_mid, sm_recv2,
    load_sem, in_sem, dsend, drecv, psend, precv, ksend, krecv, rsend, rrecv, xsend, xrecv, gsend, grecv,
    s1send, s1recv, s2send, s2recv,
):
    bi = lax.axis_index("batch")
    si = lax.axis_index("space")
    has_prev, has_next = si > 0, si < ns - 1
    prev, nxt = (bi, jnp.maximum(si - 1, 0)), (bi, jnp.minimum(si + 1, ns - 1))

    def space_peer(d):
        return (bi, lax.rem(si + d, ns))

    def batch_peer(d):
        return (lax.rem(bi + d, nb), si)

    barrier = pltpu.get_barrier_semaphore()

    def hello(peer):
        pl.semaphore_signal(barrier, inc=1, device_id=peer, device_id_type=MESH)

    def every(numbers, act):
        if len(numbers) <= 8:
            for number in numbers:
                act(number)
        else:
            def step(index, carry):
                act(index + numbers[0])
                return carry
            lax.fori_loop(0, len(numbers), step, 0)

    loads = [pltpu.make_async_copy(dens.at[:, :, z], buf.at[z], load_sem.at[z]) for z in range(2)]
    pairs = ((w1_hbm, w1), (fold_hbm, fold), (w2_hbm, w2), (b1_hbm, b1), (b2_hbm, b2), (cot_hbm, cot))
    params = [pltpu.make_async_copy(src, dst, in_sem.at[n]) for n, (src, dst) in enumerate(pairs)]
    for copy in loads + params:
        copy.start()
    hello(space_peer(1))
    hello(space_peer(ns - 1))
    every(range(2, ns - 1), lambda d: hello(space_peer(d)))
    every(range(1, nb), lambda d: hello(batch_peer(d)))
    pl.semaphore_wait(barrier, ns - 1 + nb - 1)

    def remote(src, dst, send, recv, target):
        return pltpu.make_async_remote_copy(
            src_ref=src, dst_ref=dst, send_sem=send, recv_sem=recv, device_id=target, device_id_type=MESH
        )

    dens_copies = [
        [
            remote(buf.at[1 - side, b], buf.at[2 + side, b], dsend.at[b, side], drecv.at[b, side], (nxt, prev)[side])
            for side in range(2)
        ]
        for b in range(2)
    ]
    pool_copies = [
        [
            remote(pooled.at[b], halo2.at[b, side], psend.at[b, side], precv.at[b, side], (nxt, prev)[side])
            for side in range(2)
        ]
        for b in range(2)
    ]
    back_copies = [
        [
            remote(bsend.at[b, side], brecv.at[b, side], ksend.at[b, side], krecv.at[b, side], (nxt, prev)[side])
            for side in range(2)
        ]
        for b in range(2)
    ]
    gives, takes = (has_next, has_prev), (has_prev, has_next)

    def start(copies):
        for side in range(2):
            pl.when(gives[side])(copies[side].start)

    def wait_in(copies):
        for side in range(2):
            pl.when(takes[side])(copies[side].wait_recv)

    def wait_out(copies):
        for side in range(2):
            pl.when(gives[side])(copies[side].wait_send)

    for copy in loads:
        copy.wait()
    for b in range(2):
        start(dens_copies[b])

    for side in range(2):
        def clear(side=side):
            buf[2 + side] = jnp.zeros(buf.shape[1:], BF16)
            for b in range(2):
                halo2[b, side] = jnp.zeros(halo2.shape[2:], BF16)
                brecv[b, side] = jnp.zeros(brecv.shape[2:], BF16)
        pl.when(jnp.logical_not(takes[side]))(clear)

    for copy in params:
        copy.wait()
    w1s[...] = jnp.zeros(w1s.shape, F32)
    w1s[:, 0:108] = w1[...].astype(F32)
    w1v = w1s[...].astype(BF16)
    for pos in range(8):
        wbig[pos * 32:(pos + 1) * 32, :] = dot(w1v, fold[:, pos * 256:(pos + 1) * 256]).astype(BF16)
    w2s[...] = jnp.zeros(w2s.shape, F32)
    w2s[:, 0:864] = w2[...].astype(F32)
    planes = (1, 0, 2)
    for j in range(3):
        for slot, i in enumerate(planes):
            lane = i * 288 + j * 96
            w2c[j * 64:(j + 1) * 64, slot * 96:(slot + 1) * 96] = w2s[:, lane:lane + 96].astype(BF16)
    for t4 in range(7):
        turned = w2s[:, t4 * 128:(t4 + 1) * 128].T
        for quarter in range(4):
            t = t4 * 4 + quarter
            if t < 27:
                i, j, k = t // 9, (t // 3) % 3, t % 3
                block = turned[quarter * 32:(quarter + 1) * 32, :]
                wb[j * 96 + i * 32:j * 96 + (i + 1) * 32, k * 64:(k + 1) * 64] = block.astype(BF16)
    bias1 = column_of(b1[...])
    bias1 = jnp.concatenate([bias1] * 8, axis=0)
    bias2 = column_of(b2[...])
    c9[...] = jnp.zeros(c9.shape, BF16)
    cb[...] = jnp.zeros(cb.shape, BF16)
    gs[...] = jnp.zeros(gs.shape, BF16)
    part[448:512, :] = jnp.zeros((64, 128), BF16)

    r, s = iota((256, 256), 0), iota((256, 256), 1)
    rows = (r & 192) + (r & 3) * 16 + ((r >> 3) & 7) * 2 + ((r >> 2) & 1)
    move_rows = (rows == s).astype(F32)[0:128, 0:128].astype(BF16)
    move_lanes = (r == (s & 127) * 2 + (s >> 7)).astype(F32).astype(BF16)

    def lay_out(pair, b):
        flat = buf[pair * 2:pair * 2 + 2, b].reshape(128, 256)
        moved = dot(move_rows, dot(flat, move_lanes).astype(BF16)).reshape(2, 8, 8, 256)
        gap = jnp.zeros((2, 1, 8, 256), F32)
        low = jnp.concatenate([gap, moved[:, :7]], axis=1)
        high = jnp.concatenate([moved[:, 1:], gap], axis=1)
        odd = iota(moved.shape, 2) >= 4
        beside = jnp.where(odd, low, high)
        for xg, field in enumerate((moved, beside)):
            even_y, odd_y = field[..., :128], field[..., 128:]
            for yg in range(2):
                halves = (even_y, odd_y) if yg == 0 else (after(even_y), before(odd_y))
                tile = jnp.concatenate(halves, axis=2).astype(BF16)
                for z in range(2):
                    row = ((pair * 2 + z) * 4 + xg * 2 + yg) * 16
                    for x in range(8):
                        lane = (b * 8 + x) * 128
                        cols1[row:row + 16, lane:lane + 128] = tile[z, x]

    for b in range(2):
        lay_out(0, b)

    def fill(target, row, height, b, field, flip):
        for x in range(8):
            lane = (b * 10 + 1 + x) * 128
            tile = field[:, x * 128:(x + 1) * 128]
            shifts = (before(tile), tile, after(tile))
            for k in range(3):
                piece = shifts[2 - k] if flip else shifts[k]
                target[row + k * height:row + (k + 1) * height, lane:lane + 128] = piece.astype(BF16)

    for b in range(2):
        wait_in(dens_copies[b])
        lay_out(1, b)
        for q in range(4):
            lane = b * 1024 + q * 256
            pre = dot(wbig[...], cols1[:, lane:lane + 256]) + bias1
            sig = sigmoid(pre)
            act = pre * sig
            d1[:, lane:lane + 256] = sig + act - act * sig
            total = act[0:32]
            for pos in range(1, 8):
                total = total + act[pos * 32:(pos + 1) * 32]
            pooled[b, :, q * 256:(q + 1) * 256] = (total * 0.125).astype(BF16)
        start(pool_copies[b])
    for b in range(2):
        fill(c9, 0, 32, b, pooled[b].astype(F32), False)
        acc2[b] = dot(w2c[:, 0:96], c9[0:96, b * 1280:(b + 1) * 1280])
        trans[b] = cot[b].astype(F32)

    for b in range(2):
        wait_in(pool_copies[b])
        for side in range(2):
            fill(c9, 96 + side * 96, 32, b, halo2[b, side].astype(F32), False)
        acc = acc2[b] + dot(w2c[:, 96:288], c9[96:288, b * 1280:(b + 1) * 1280])
        pre = acc[0:64, 0:1024] + acc[64:128, 128:1152] + acc[128:192, 256:1280] + bias2
        sig = sigmoid(pre)
        act = pre * sig
        slope = sig + act - act * sig
        grads = []
        for x in range(8):
            grads.append(trans[b, pl.ds(x, 64, stride=8), :] * slope[:, x * 128:(x + 1) * 128])
        grad = jnp.concatenate(grads, axis=1).astype(BF16)
        for j in range(3):
            lane = b * 1280 + j * 128
            gs[j * 64:(j + 1) * 64, lane:lane + 1024] = grad
        grad = grad.astype(F32)
        fill(cb, 0, 64, b, grad, True)
        acc = dot(wb[...], cb[:, b * 1280:(b + 1) * 1280])
        give = acc[0:96, 256:1280] + acc[96:192, 128:1152] + acc[192:288, 0:1024]
        bsend[b, 1] = give[0:32].astype(BF16)
        bsend[b, 0] = give[64:96].astype(BF16)
        start(back_copies[b])
        bown[:, b * 1024:(b + 1) * 1024] = give[32:64]
        acts[b] = act

    total = dot_nt(gs[...], c9[...])
    for j in range(3):
        for slot, i in enumerate(planes):
            lane = i * 288 + j * 96
            w2s[:, lane:lane + 96] = total[j * 64:(j + 1) * 64, slot * 96:(slot + 1) * 96]
    for t in range(7):
        part[t * 64:(t + 1) * 64, :] = w2s[:, t * 128:(t + 1) * 128].astype(BF16)

    size = 512 // ns

    def chunk(index):
        return pl.ds(pl.multiple_of(index * size, size), size)

    def rs_copy(d):
        return remote(part.at[chunk(lax.rem(si + d, ns))], rs_recv.at[d], rsend.at[d], rrecv.at[d], space_peer(d))

    def bx_copy(d):
        return remote(mine.at[0], bx_recv.at[bi], xsend.at[d], xrecv.at[d], batch_peer(d))

    def ag_copy(d):
        return remote(mine.at[1], full.at[chunk(si)], gsend.at[d], grecv.at[d], space_peer(d))

    def s1_copy(d):
        return remote(small, sm_recv.at[si], s1send.at[d], s1recv.at[d], space_peer(d))

    def s2_copy(d):
        return remote(sm_mid, sm_recv2.at[bi], s2send.at[d], s2recv.at[d], batch_peer(d))

    def each(count, make, act):
        every(range(1, count), lambda d: act(make(d)))

    def go(copy):
        copy.start()

    def arrive(copy):
        copy.wait_recv()

    def leave(copy):
        copy.wait_send()

    def in_order(terms, count):
        total = terms[0].astype(F32)
        for index in range(1, count):
            total = total + terms[index].astype(F32)
        return total

    each(ns, rs_copy, go)

    gb2 = jnp.sum(gs[64:128, :].astype(F32), axis=1, keepdims=True)
    for b in range(2):
        for x in range(8):
            trans[b, pl.ds(x, 64, stride=8), :] = acts[b, :, x * 128:(x + 1) * 128]
        feat[b] = trans[b].astype(BF16)

    gb1 = jnp.zeros((32, 256), F32)
    for b in range(2):
        wait_in(back_copies[b])
        for q in range(4):
            lane = b * 1024 + q * 256
            near = brecv[b, :, :, q * 256:(q + 1) * 256].astype(F32)
            back = (bown[:, lane:lane + 256] + near[0] + near[1]) * 0.125
            for pos in range(8):
                piece = (back * d1[pos * 32:(pos + 1) * 32, lane:lane + 256]).astype(BF16)
                gf[pos * 32:(pos + 1) * 32, lane:lane + 256] = piece
                gb1 = gb1 + piece.astype(F32)
        term = dot_nt(gf[:, b * 1024:(b + 1) * 1024], cols1[:, b * 1024:(b + 1) * 1024])
        if b == 0:
            held[...] = term
    gram = held[...] + term
    high = gram.astype(BF16)
    low = (gram - high.astype(F32)).astype(BF16)
    folded = jnp.zeros((64, 128), F32)
    for pos in range(8):
        both = jnp.concatenate([high[pos * 32:(pos + 1) * 32], low[pos * 32:(pos + 1) * 32]], axis=0)
        folded = folded + dot_nt(both, fold[:, pos * 256:(pos + 1) * 256])
    lane = iota((32, 128), 1)
    sums = folded[0:32] + folded[32:64]
    sums = jnp.where(lane == 108, jnp.sum(gb1, axis=1, keepdims=True), sums)
    sums = jnp.where(lane == 109, gb2[0:32], sums)
    small[...] = jnp.where(lane == 110, gb2[32:64], sums).astype(BF16)
    each(ns, s1_copy, go)

    each(ns, rs_copy, arrive)
    total = part[chunk(si), :].astype(F32)
    for d in range(1, ns):
        total = total + rs_recv[d].astype(F32)
    total = total.astype(BF16)
    mine[0] = total
    bx_recv[bi] = total
    each(nb, bx_copy, go)

    each(ns, s1_copy, arrive)
    sm_recv[si] = small[...]
    total = in_order(sm_recv, ns).astype(BF16)
    sm_mid[...] = total
    sm_recv2[bi] = total
    each(nb, s2_copy, go)

    each(nb, bx_copy, arrive)
    total = in_order(bx_recv, nb).astype(BF16)
    mine[1] = total
    full[chunk(si), :] = total
    each(ns, ag_copy, go)

    each(nb, s2_copy, arrive)
    total = in_order(sm_recv2, nb)
    gw1_out[...] = total[:, 0:108]
    gb1_out[...] = row_of(total[:, 108:109])
    gb2_out[...] = row_of(jnp.concatenate([total[:, 109:110], total[:, 110:111]], axis=0))

    for b in range(2):
        wait_out(dens_copies[b])
        wait_out(pool_copies[b])
        wait_out(back_copies[b])
    each(ns, rs_copy, leave)
    each(nb, bx_copy, leave)
    each(ns, s1_copy, leave)
    each(nb, s2_copy, leave)
    each(ns, ag_copy, arrive)
    for t in range(7):
        width = min(128, 864 - t * 128)
        gw2_out[:, t * 128:t * 128 + width] = full[t * 64:(t + 1) * 64, 0:width].astype(F32)

    each(ns, ag_copy, leave)


def hand_out(*refs):
    held, results, sems = refs[0:5], refs[5:10], refs[10]
    outward = [pltpu.make_async_copy(held[n], results[n], sems.at[n]) for n in range(5)]
    for copy in outward:
        copy.start()
    for copy in outward:
        copy.wait()


def body(nb, ns, density, w_first, b_first, w_second, b_second, cotangent):
    vmem = pl.BlockSpec(memory_space=pltpu.VMEM)
    hbm = pl.BlockSpec(memory_space=pltpu.HBM)
    dma = pltpu.SemaphoreType.DMA
    size = 512 // ns
    shapes = (
        jax.ShapeDtypeStruct((2, 512, 128), BF16),
        jax.ShapeDtypeStruct((32, 108), F32),
        jax.ShapeDtypeStruct((1, 32), F32),
        jax.ShapeDtypeStruct((64, 864), F32),
        jax.ShapeDtypeStruct((1, 64), F32),
    )
    held = pl.pallas_call(
        functools.partial(kernel, nb, ns),
        out_shape=tuple(pltpu.VMEM(one.shape, one.dtype) for one in shapes),
        in_specs=[hbm] * 7,
        out_specs=(vmem,) * 5,
        scratch_shapes=[
            pltpu.VMEM((32, 108), BF16),
            pltpu.VMEM((1, 32), F32),
            pltpu.VMEM((64, 864), BF16),
            pltpu.VMEM((1, 64), F32),
            pltpu.VMEM((2, 512, 128), BF16),
            pltpu.VMEM((128, 2048), BF16),
            pltpu.VMEM((4, 2, 4, 16, 256), BF16),
            pltpu.VMEM((256, 2048), BF16),
            pltpu.VMEM((256, 256), BF16),
            pltpu.VMEM((256, 2048), F32),
            pltpu.VMEM((32, 128), F32),
            pltpu.VMEM((64, 896), F32),
            pltpu.VMEM((192, 288), BF16),
            pltpu.VMEM((288, 192), BF16),
            pltpu.VMEM((2, 32, 1024), BF16),
            pltpu.VMEM((2, 2, 32, 1024), BF16),
            pltpu.VMEM((288, 2560), BF16),
            pltpu.VMEM((2, 192, 1280), F32),
            pltpu.VMEM((2, 512, 128), F32),
            pltpu.VMEM((2, 64, 1024), F32),
            pltpu.VMEM((256, 256), F32),
            pltpu.VMEM((192, 2560), BF16),
            pltpu.VMEM((192, 2560), BF16),
            pltpu.VMEM((2, 2, 32, 1024), BF16),
            pltpu.VMEM((2, 2, 32, 1024), BF16),
            pltpu.VMEM((32, 2048), F32),
            pltpu.VMEM((256, 2048), BF16),
            pltpu.VMEM((512, 128), BF16),
            pltpu.VMEM((ns, size, 128), BF16),
            pltpu.VMEM((2, size, 128), BF16),
            pltpu.VMEM((nb, size, 128), BF16),
            pltpu.VMEM((512, 128), BF16),
            pltpu.VMEM((32, 128), BF16),
            pltpu.VMEM((ns, 32, 128), BF16),
            pltpu.VMEM((32, 128), BF16),
            pltpu.VMEM((nb, 32, 128), BF16),
            dma((2,)), dma((6,)), dma((2, 2)), dma((2, 2)),
            dma((2, 2)), dma((2, 2)), dma((2, 2)), dma((2, 2)),
            dma((ns,)), dma((ns,)), dma((nb,)), dma((nb,)), dma((ns,)), dma((ns,)),
            dma((ns,)), dma((ns,)), dma((nb,)), dma((nb,)),
        ],
        compiler_params=pltpu.CompilerParams(
            collective_id=0, has_side_effects=True, vmem_limit_bytes=40 * 1024 * 1024
        ),
        cost_estimate=pl.CostEstimate(flops=1 << 30, bytes_accessed=1 << 21, transcendentals=1 << 20),
    )(*[
        pltpu.with_memory_space_constraint(one, pltpu.HBM)
        for one in (
            density, w_first, b_first.reshape(1, 32), w_second, b_second.reshape(1, 64), cotangent.reshape(2, 512, 128),
            jnp.asarray(fold_matrix(), BF16),
        )
    ])
    feat, gw1, gb1, gw2, gb2 = pl.pallas_call(
        hand_out,
        out_shape=shapes,
        in_specs=[vmem] * 5,
        out_specs=(hbm,) * 5,
        scratch_shapes=[dma((5,))],
        compiler_params=pltpu.CompilerParams(vmem_limit_bytes=8 * 1024 * 1024),
    )(*held)
    return feat.reshape(cotangent.shape), gw1, gb1.reshape(32), gw2, gb2.reshape(64)


def solution(mesh):
    data = P("batch", None, "space", None, None)
    return jax.shard_map(
        functools.partial(body, mesh.shape["batch"], mesh.shape["space"]),
        mesh=mesh,
        in_specs=(data, P(), P(), P(), P(), data),
        out_specs=(data, P(), P(), P(), P()),
        check_vma=False,
    )
```

```python
import functools

import jax
import jax.numpy as jnp
import numpy as np
from jax import lax
from jax.experimental import pallas as pl
from jax.experimental.pallas import tpu as pltpu
from jax.sharding import PartitionSpec as P

F32 = jnp.float32
BF16 = jnp.bfloat16
MESH = pl.DeviceIdType.MESH
NT = (((1,), (1,)), ((), ()))


def fold_matrix():
    fold = np.zeros((128, 8, 256), np.float32)

    def coordinate(group, parity):
        return 1 + parity if group == 0 else (0 if parity == 1 else 3)

    planes = (1, 2, 0, 3)
    for row in range(256):
        zi, xg, yg = row >> 6, (row >> 5) & 1, (row >> 4) & 1
        yp, xp, c = (row >> 3) & 1, (row >> 2) & 1, row & 3
        zz, xx, yy = planes[zi], coordinate(xg, xp), coordinate(yg, yp)
        for pos in range(8):
            i, j, k = zz - (pos >> 2), xx - ((pos >> 1) & 1), yy - (pos & 1)
            if 0 <= i < 3 and 0 <= j < 3 and 0 <= k < 3:
                fold[((i * 3 + j) * 3 + k) * 4 + c, pos, row] = 1
    return fold.reshape(128, 2048)


def iota(shape, axis):
    return lax.broadcasted_iota(jnp.int32, shape, axis)


def sigmoid(value):
    return 0.5 + 0.5 * jnp.tanh(0.5 * value)


def column_of(row):
    size = row.shape[1]
    eye = iota((size, size), 0) == iota((size, size), 1)
    return jnp.sum(jnp.where(eye, row, 0.0), axis=1, keepdims=True)


def row_of(column):
    size = column.shape[0]
    eye = iota((size, size), 0) == iota((size, size), 1)
    return jnp.sum(jnp.where(eye, column, 0.0), axis=0, keepdims=True)


def dot(a, b):
    return jnp.dot(a, b, preferred_element_type=F32)


def dot_nt(a, b):
    return lax.dot_general(a, b, NT, preferred_element_type=F32)


def before(tile):
    axis = tile.ndim - 1
    return jnp.where(iota(tile.shape, axis) == 0, 0.0, pltpu.roll(tile, 1, axis))


def after(tile):
    axis = tile.ndim - 1
    return jnp.where(iota(tile.shape, axis) == 127, 0.0, pltpu.roll(tile, 127, axis))


def kernel(
    nb, ns,
    dens, w1_hbm, b1_hbm, w2_hbm, b2_hbm, cot_hbm, fold_hbm,
    feat, gw1_out, gb1_out, gw2_out, gb2_out,
    w1, b1, w2, b2, cot, fold, buf, cols1, wbig, d1, w1s, w2s, w2c, wb, pooled, halo2, c9, acc2, trans, acts, held, gs, cb, bsend, brecv, bown, gf,
    part, rs_recv, mine, bx_recv, full, small, sm_recv, sm_mid, sm_recv2,
    load_sem, in_sem, dsend, drecv, psend, precv, ksend, krecv, rsend, rrecv, xsend, xrecv, gsend, grecv,
    s1send, s1recv, s2send, s2recv,
):
    bi = lax.axis_index("batch")
    si = lax.axis_index("space")
    has_prev, has_next = si > 0, si < ns - 1
    prev, nxt = (bi, jnp.maximum(si - 1, 0)), (bi, jnp.minimum(si + 1, ns - 1))

    def space_peer(d):
        return (bi, lax.rem(si + d, ns))

    def batch_peer(d):
        return (lax.rem(bi + d, nb), si)

    barrier = pltpu.get_barrier_semaphore()

    def hello(peer):
        pl.semaphore_signal(barrier, inc=1, device_id=peer, device_id_type=MESH)

    def every(numbers, act):
        if len(numbers) <= 8:
            for number in numbers:
                act(number)
        else:
            def step(index, carry):
                act(index + numbers[0])
                return carry
            lax.fori_loop(0, len(numbers), step, 0)

    loads = [pltpu.make_async_copy(dens.at[:, :, z], buf.at[z], load_sem.at[z]) for z in range(2)]
    pairs = ((w1_hbm, w1), (fold_hbm, fold), (w2_hbm, w2), (b1_hbm, b1), (b2_hbm, b2), (cot_hbm, cot))
    params = [pltpu.make_async_copy(src, dst, in_sem.at[n]) for n, (src, dst) in enumerate(pairs)]
    for copy in loads + params:
        copy.start()
    hello(space_peer(1))
    hello(space_peer(ns - 1))
    every(range(2, ns - 1), lambda d: hello(space_peer(d)))
    every(range(1, nb), lambda d: hello(batch_peer(d)))
    pl.semaphore_wait(barrier, ns - 1 + nb - 1)

    def remote(src, dst, send, recv, target):
        return pltpu.make_async_remote_copy(
            src_ref=src, dst_ref=dst, send_sem=send, recv_sem=recv, device_id=target, device_id_type=MESH
        )

    dens_copies = [
        [
            remote(buf.at[1 - side, b], buf.at[2 + side, b], dsend.at[b, side], drecv.at[b, side], (nxt, prev)[side])
            for side in range(2)
        ]
        for b in range(2)
    ]
    pool_copies = [
        [
            remote(pooled.at[b], halo2.at[b, side], psend.at[b, side], precv.at[b, side], (nxt, prev)[side])
            for side in range(2)
        ]
        for b in range(2)
    ]
    back_copies = [
        [
            remote(bsend.at[b, side], brecv.at[b, side], ksend.at[b, side], krecv.at[b, side], (nxt, prev)[side])
            for side in range(2)
        ]
        for b in range(2)
    ]
    gives, takes = (has_next, has_prev), (has_prev, has_next)

    def start(copies):
        for side in range(2):
            pl.when(gives[side])(copies[side].start)

    def wait_in(copies):
        for side in range(2):
            pl.when(takes[side])(copies[side].wait_recv)

    def wait_out(copies):
        for side in range(2):
            pl.when(gives[side])(copies[side].wait_send)

    for copy in loads:
        copy.wait()
    for b in range(2):
        start(dens_copies[b])

    for side in range(2):
        def clear(side=side):
            buf[2 + side] = jnp.zeros(buf.shape[1:], BF16)
            for b in range(2):
                halo2[b, side] = jnp.zeros(halo2.shape[2:], BF16)
                brecv[b, side] = jnp.zeros(brecv.shape[2:], BF16)
        pl.when(jnp.logical_not(takes[side]))(clear)

    for copy in params:
        copy.wait()
    w1s[...] = jnp.zeros(w1s.shape, F32)
    w1s[:, 0:108] = w1[...].astype(F32)
    w1v = w1s[...].astype(BF16)
    for pos in range(8):
        wbig[pos * 32:(pos + 1) * 32, :] = dot(w1v, fold[:, pos * 256:(pos + 1) * 256]).astype(BF16)
    w2s[...] = jnp.zeros(w2s.shape, F32)
    w2s[:, 0:864] = w2[...].astype(F32)
    planes = (1, 0, 2)
    for j in range(3):
        for slot, i in enumerate(planes):
            lane = i * 288 + j * 96
            w2c[j * 64:(j + 1) * 64, slot * 96:(slot + 1) * 96] = w2s[:, lane:lane + 96].astype(BF16)
    for t4 in range(7):
        turned = w2s[:, t4 * 128:(t4 + 1) * 128].T
        for quarter in range(4):
            t = t4 * 4 + quarter
            if t < 27:
                i, j, k = t // 9, (t // 3) % 3, t % 3
                block = turned[quarter * 32:(quarter + 1) * 32, :]
                wb[j * 96 + i * 32:j * 96 + (i + 1) * 32, k * 64:(k + 1) * 64] = block.astype(BF16)
    bias1 = column_of(b1[...])
    bias1 = jnp.concatenate([bias1] * 8, axis=0)
    bias2 = column_of(b2[...])
    c9[...] = jnp.zeros(c9.shape, BF16)
    cb[...] = jnp.zeros(cb.shape, BF16)
    gs[...] = jnp.zeros(gs.shape, BF16)
    part[448:512, :] = jnp.zeros((64, 128), BF16)

    r, s = iota((256, 256), 0), iota((256, 256), 1)
    rows = (r & 192) + (r & 3) * 16 + ((r >> 3) & 7) * 2 + ((r >> 2) & 1)
    move_rows = (rows == s).astype(F32)[0:128, 0:128].astype(BF16)
    move_lanes = (r == (s & 127) * 2 + (s >> 7)).astype(F32).astype(BF16)

    def lay_out(pair, b):
        flat = buf[pair * 2:pair * 2 + 2, b].reshape(128, 256)
        moved = dot(move_rows, dot(flat, move_lanes).astype(BF16)).reshape(2, 8, 8, 256)
        gap = jnp.zeros((2, 1, 8, 256), F32)
        low = jnp.concatenate([gap, moved[:, :7]], axis=1)
        high = jnp.concatenate([moved[:, 1:], gap], axis=1)
        odd = iota(moved.shape, 2) >= 4
        beside = jnp.where(odd, low, high)
        for xg, field in enumerate((moved, beside)):
            even_y, odd_y = field[..., :128], field[..., 128:]
            for yg in range(2):
                halves = (even_y, odd_y) if yg == 0 else (after(even_y), before(odd_y))
                tile = jnp.concatenate(halves, axis=2).astype(BF16)
                for z in range(2):
                    row = ((pair * 2 + z) * 4 + xg * 2 + yg) * 16
                    for x in range(8):
                        lane = (b * 8 + x) * 128
                        cols1[row:row + 16, lane:lane + 128] = tile[z, x]

    for b in range(2):
        lay_out(0, b)

    def fill(target, row, height, b, field, flip):
        for x in range(8):
            lane = (b * 10 + 1 + x) * 128
            tile = field[:, x * 128:(x + 1) * 128]
            shifts = (before(tile), tile, after(tile))
            for k in range(3):
                piece = shifts[2 - k] if flip else shifts[k]
                target[row + k * height:row + (k + 1) * height, lane:lane + 128] = piece.astype(BF16)

    for b in range(2):
        wait_in(dens_copies[b])
        lay_out(1, b)
        for q in range(4):
            lane = b * 1024 + q * 256
            pre = dot(wbig[...], cols1[:, lane:lane + 256]) + bias1
            sig = sigmoid(pre)
            act = pre * sig
            d1[:, lane:lane + 256] = sig + act - act * sig
            total = act[0:32]
            for pos in range(1, 8):
                total = total + act[pos * 32:(pos + 1) * 32]
            pooled[b, :, q * 256:(q + 1) * 256] = (total * 0.125).astype(BF16)
        start(pool_copies[b])
    for b in range(2):
        fill(c9, 0, 32, b, pooled[b].astype(F32), False)
        acc2[b] = dot(w2c[:, 0:96], c9[0:96, b * 1280:(b + 1) * 1280])
        trans[b] = cot[b].astype(F32)

    for b in range(2):
        wait_in(pool_copies[b])
        for side in range(2):
            fill(c9, 96 + side * 96, 32, b, halo2[b, side].astype(F32), False)
        acc = acc2[b] + dot(w2c[:, 96:288], c9[96:288, b * 1280:(b + 1) * 1280])
        pre = acc[0:64, 0:1024] + acc[64:128, 128:1152] + acc[128:192, 256:1280] + bias2
        sig = sigmoid(pre)
        act = pre * sig
        slope = sig + act - act * sig
        grads = []
        for x in range(8):
            grads.append(trans[b, pl.ds(x, 64, stride=8), :] * slope[:, x * 128:(x + 1) * 128])
        grad = jnp.concatenate(grads, axis=1).astype(BF16)
        for j in range(3):
            lane = b * 1280 + j * 128
            gs[j * 64:(j + 1) * 64, lane:lane + 1024] = grad
        grad = grad.astype(F32)
        fill(cb, 0, 64, b, grad, True)
        acc = dot(wb[...], cb[:, b * 1280:(b + 1) * 1280])
        give = acc[0:96, 256:1280] + acc[96:192, 128:1152] + acc[192:288, 0:1024]
        bsend[b, 1] = give[0:32].astype(BF16)
        bsend[b, 0] = give[64:96].astype(BF16)
        start(back_copies[b])
        bown[:, b * 1024:(b + 1) * 1024] = give[32:64]
        acts[b] = act

    total = dot_nt(gs[...], c9[...])
    for j in range(3):
        for slot, i in enumerate(planes):
            lane = i * 288 + j * 96
            w2s[:, lane:lane + 96] = total[j * 64:(j + 1) * 64, slot * 96:(slot + 1) * 96]
    for t in range(7):
        part[t * 64:(t + 1) * 64, :] = w2s[:, t * 128:(t + 1) * 128].astype(BF16)

    size = 512 // ns

    def chunk(index):
        return pl.ds(pl.multiple_of(index * size, size), size)

    def rs_copy(d):
        return remote(part.at[chunk(lax.rem(si + d, ns))], rs_recv.at[d], rsend.at[d], rrecv.at[d], space_peer(d))

    def bx_copy(d):
        return remote(mine.at[0], bx_recv.at[bi], xsend.at[d], xrecv.at[d], batch_peer(d))

    def ag_copy(d):
        return remote(mine.at[1], full.at[chunk(si)], gsend.at[d], grecv.at[d], space_peer(d))

    def s1_copy(d):
        return remote(small, sm_recv.at[si], s1send.at[d], s1recv.at[d], space_peer(d))

    def s2_copy(d):
        return remote(sm_mid, sm_recv2.at[bi], s2send.at[d], s2recv.at[d], batch_peer(d))

    def each(count, make, act):
        every(range(1, count), lambda d: act(make(d)))

    def go(copy):
        copy.start()

    def arrive(copy):
        copy.wait_recv()

    def leave(copy):
        copy.wait_send()

    def in_order(terms, count):
        total = terms[0].astype(F32)
        for index in range(1, count):
            total = total + terms[index].astype(F32)
        return total

    live = -(-448 // size)

    def rs_go(d):
        pl.when(lax.rem(si + d, ns) < live)(rs_copy(d).start)

    def rs_leave(d):
        pl.when(lax.rem(si + d, ns) < live)(rs_copy(d).wait_send)

    def ag_arrive(d):
        pl.when(lax.rem(si + ns - d, ns) < live)(ag_copy(d).wait_recv)

    every(range(1, ns), rs_go)

    gb2 = jnp.sum(gs[64:128, :].astype(F32), axis=1, keepdims=True)
    for b in range(2):
        for x in range(8):
            trans[b, pl.ds(x, 64, stride=8), :] = acts[b, :, x * 128:(x + 1) * 128]
        feat[b] = trans[b].astype(BF16)

    gb1 = jnp.zeros((32, 256), F32)
    for b in range(2):
        wait_in(back_copies[b])
        for q in range(4):
            lane = b * 1024 + q * 256
            near = brecv[b, :, :, q * 256:(q + 1) * 256].astype(F32)
            back = (bown[:, lane:lane + 256] + near[0] + near[1]) * 0.125
            for pos in range(8):
                piece = (back * d1[pos * 32:(pos + 1) * 32, lane:lane + 256]).astype(BF16)
                gf[pos * 32:(pos + 1) * 32, lane:lane + 256] = piece
                gb1 = gb1 + piece.astype(F32)
        term = dot_nt(gf[:, b * 1024:(b + 1) * 1024], cols1[:, b * 1024:(b + 1) * 1024])
        if b == 0:
            held[...] = term
    gram = held[...] + term
    high = gram.astype(BF16)
    low = (gram - high.astype(F32)).astype(BF16)
    folded = jnp.zeros((64, 128), F32)
    for pos in range(8):
        both = jnp.concatenate([high[pos * 32:(pos + 1) * 32], low[pos * 32:(pos + 1) * 32]], axis=0)
        folded = folded + dot_nt(both, fold[:, pos * 256:(pos + 1) * 256])
    lane = iota((32, 128), 1)
    sums = folded[0:32] + folded[32:64]
    sums = jnp.where(lane == 108, jnp.sum(gb1, axis=1, keepdims=True), sums)
    sums = jnp.where(lane == 109, gb2[0:32], sums)
    small[...] = jnp.where(lane == 110, gb2[32:64], sums).astype(BF16)
    each(ns, s1_copy, go)

    @pl.when(si < live)
    def space_sum():
        each(ns, rs_copy, arrive)
        total = part[chunk(si), :].astype(F32)
        for d in range(1, ns):
            total = total + rs_recv[d].astype(F32)
        total = total.astype(BF16)
        mine[0] = total
        bx_recv[bi] = total
        each(nb, bx_copy, go)

    each(ns, s1_copy, arrive)
    sm_recv[si] = small[...]
    total = in_order(sm_recv, ns).astype(BF16)
    sm_mid[...] = total
    sm_recv2[bi] = total
    each(nb, s2_copy, go)

    @pl.when(si < live)
    def batch_sum():
        each(nb, bx_copy, arrive)
        total = in_order(bx_recv, nb).astype(BF16)
        mine[1] = total
        full[chunk(si), :] = total
        each(ns, ag_copy, go)

    each(nb, s2_copy, arrive)
    total = in_order(sm_recv2, nb)
    gw1_out[...] = total[:, 0:108]
    gb1_out[...] = row_of(total[:, 108:109])
    gb2_out[...] = row_of(jnp.concatenate([total[:, 109:110], total[:, 110:111]], axis=0))

    for b in range(2):
        wait_out(dens_copies[b])
        wait_out(pool_copies[b])
        wait_out(back_copies[b])
    every(range(1, ns), rs_leave)
    each(ns, s1_copy, leave)
    each(nb, s2_copy, leave)
    every(range(1, ns), ag_arrive)
    for t in range(7):
        width = min(128, 864 - t * 128)
        gw2_out[:, t * 128:t * 128 + width] = full[t * 64:(t + 1) * 64, 0:width].astype(F32)

    @pl.when(si < live)
    def done():
        each(nb, bx_copy, leave)
        each(ns, ag_copy, leave)


def hand_out(*refs):
    held, results, sems = refs[0:5], refs[5:10], refs[10]
    outward = [pltpu.make_async_copy(held[n], results[n], sems.at[n]) for n in range(5)]
    for copy in outward:
        copy.start()
    for copy in outward:
        copy.wait()


def body(nb, ns, density, w_first, b_first, w_second, b_second, cotangent):
    vmem = pl.BlockSpec(memory_space=pltpu.VMEM)
    hbm = pl.BlockSpec(memory_space=pltpu.HBM)
    dma = pltpu.SemaphoreType.DMA
    size = 512 // ns
    shapes = (
        jax.ShapeDtypeStruct((2, 512, 128), BF16),
        jax.ShapeDtypeStruct((32, 108), F32),
        jax.ShapeDtypeStruct((1, 32), F32),
        jax.ShapeDtypeStruct((64, 864), F32),
        jax.ShapeDtypeStruct((1, 64), F32),
    )
    held = pl.pallas_call(
        functools.partial(kernel, nb, ns),
        out_shape=tuple(pltpu.VMEM(one.shape, one.dtype) for one in shapes),
        in_specs=[hbm] * 7,
        out_specs=(vmem,) * 5,
        scratch_shapes=[
            pltpu.VMEM((32, 108), BF16),
            pltpu.VMEM((1, 32), F32),
            pltpu.VMEM((64, 864), BF16),
            pltpu.VMEM((1, 64), F32),
            pltpu.VMEM((2, 512, 128), BF16),
            pltpu.VMEM((128, 2048), BF16),
            pltpu.VMEM((4, 2, 4, 16, 256), BF16),
            pltpu.VMEM((256, 2048), BF16),
            pltpu.VMEM((256, 256), BF16),
            pltpu.VMEM((256, 2048), F32),
            pltpu.VMEM((32, 128), F32),
            pltpu.VMEM((64, 896), F32),
            pltpu.VMEM((192, 288), BF16),
            pltpu.VMEM((288, 192), BF16),
            pltpu.VMEM((2, 32, 1024), BF16),
            pltpu.VMEM((2, 2, 32, 1024), BF16),
            pltpu.VMEM((288, 2560), BF16),
            pltpu.VMEM((2, 192, 1280), F32),
            pltpu.VMEM((2, 512, 128), F32),
            pltpu.VMEM((2, 64, 1024), F32),
            pltpu.VMEM((256, 256), F32),
            pltpu.VMEM((192, 2560), BF16),
            pltpu.VMEM((192, 2560), BF16),
            pltpu.VMEM((2, 2, 32, 1024), BF16),
            pltpu.VMEM((2, 2, 32, 1024), BF16),
            pltpu.VMEM((32, 2048), F32),
            pltpu.VMEM((256, 2048), BF16),
            pltpu.VMEM((512, 128), BF16),
            pltpu.VMEM((ns, size, 128), BF16),
            pltpu.VMEM((2, size, 128), BF16),
            pltpu.VMEM((nb, size, 128), BF16),
            pltpu.VMEM((512, 128), BF16),
            pltpu.VMEM((32, 128), BF16),
            pltpu.VMEM((ns, 32, 128), BF16),
            pltpu.VMEM((32, 128), BF16),
            pltpu.VMEM((nb, 32, 128), BF16),
            dma((2,)), dma((6,)), dma((2, 2)), dma((2, 2)),
            dma((2, 2)), dma((2, 2)), dma((2, 2)), dma((2, 2)),
            dma((ns,)), dma((ns,)), dma((nb,)), dma((nb,)), dma((ns,)), dma((ns,)),
            dma((ns,)), dma((ns,)), dma((nb,)), dma((nb,)),
        ],
        compiler_params=pltpu.CompilerParams(
            collective_id=0, has_side_effects=True, vmem_limit_bytes=40 * 1024 * 1024
        ),
        cost_estimate=pl.CostEstimate(flops=1 << 30, bytes_accessed=1 << 21, transcendentals=1 << 20),
    )(*[
        pltpu.with_memory_space_constraint(one, pltpu.HBM)
        for one in (
            density, w_first, b_first.reshape(1, 32), w_second, b_second.reshape(1, 64), cotangent.reshape(2, 512, 128),
            jnp.asarray(fold_matrix(), BF16),
        )
    ])
    feat, gw1, gb1, gw2, gb2 = pl.pallas_call(
        hand_out,
        out_shape=shapes,
        in_specs=[vmem] * 5,
        out_specs=(hbm,) * 5,
        scratch_shapes=[dma((5,))],
        compiler_params=pltpu.CompilerParams(vmem_limit_bytes=8 * 1024 * 1024),
    )(*held)
    return feat.reshape(cotangent.shape), gw1, gb1.reshape(32), gw2, gb2.reshape(64)


def solution(mesh):
    data = P("batch", None, "space", None, None)
    return jax.shard_map(
        functools.partial(body, mesh.shape["batch"], mesh.shape["space"]),
        mesh=mesh,
        in_specs=(data, P(), P(), P(), P(), data),
        out_specs=(data, P(), P(), P(), P()),
        check_vma=False,
    )
```

```python
import functools

import jax
import jax.numpy as jnp
import numpy as np
from jax import lax
from jax.experimental import pallas as pl
from jax.experimental.pallas import tpu as pltpu
from jax.sharding import PartitionSpec as P

F32 = jnp.float32
BF16 = jnp.bfloat16
MESH = pl.DeviceIdType.MESH
NT = (((1,), (1,)), ((), ()))


def fold_matrix():
    fold = np.zeros((128, 8, 256), np.float32)

    def coordinate(group, parity):
        return 1 + parity if group == 0 else (0 if parity == 1 else 3)

    planes = (1, 2, 0, 3)
    for row in range(256):
        zi, xg, yg = row >> 6, (row >> 5) & 1, (row >> 4) & 1
        yp, xp, c = (row >> 3) & 1, (row >> 2) & 1, row & 3
        zz, xx, yy = planes[zi], coordinate(xg, xp), coordinate(yg, yp)
        for pos in range(8):
            i, j, k = zz - (pos >> 2), xx - ((pos >> 1) & 1), yy - (pos & 1)
            if 0 <= i < 3 and 0 <= j < 3 and 0 <= k < 3:
                fold[((i * 3 + j) * 3 + k) * 4 + c, pos, row] = 1
    return fold.reshape(128, 2048)


def iota(shape, axis):
    return lax.broadcasted_iota(jnp.int32, shape, axis)


def sigmoid(value):
    return 0.5 + 0.5 * jnp.tanh(0.5 * value)


def column_of(row):
    size = row.shape[1]
    eye = iota((size, size), 0) == iota((size, size), 1)
    return jnp.sum(jnp.where(eye, row, 0.0), axis=1, keepdims=True)


def row_of(column):
    size = column.shape[0]
    eye = iota((size, size), 0) == iota((size, size), 1)
    return jnp.sum(jnp.where(eye, column, 0.0), axis=0, keepdims=True)


def dot(a, b):
    return jnp.dot(a, b, preferred_element_type=F32)


def dot_nt(a, b):
    return lax.dot_general(a, b, NT, preferred_element_type=F32)


def before(tile):
    axis = tile.ndim - 1
    return jnp.where(iota(tile.shape, axis) == 0, 0.0, pltpu.roll(tile, 1, axis))


def after(tile):
    axis = tile.ndim - 1
    return jnp.where(iota(tile.shape, axis) == 127, 0.0, pltpu.roll(tile, 127, axis))


def kernel(
    nb, ns,
    dens, w1_hbm, b1_hbm, w2_hbm, b2_hbm, cot_hbm, fold_hbm,
    feat, gw1_out, gb1_out, gw2_out, gb2_out,
    w1, b1, w2, b2, cot, fold, buf, cols1, wbig, d1, w1s, w2s, w2c, wb, pooled, halo2, c9, acc2, trans, acts, held, gs, cb, bsend, brecv, bown, gf,
    part, rs_recv, mine, bx_recv, full, small, sm_recv, sm_mid, sm_recv2,
    load_sem, in_sem, dsend, drecv, psend, precv, ksend, krecv, rsend, rrecv, xsend, xrecv, gsend, grecv,
    s1send, s1recv, s2send, s2recv,
):
    bi = lax.axis_index("batch")
    si = lax.axis_index("space")
    has_prev, has_next = si > 0, si < ns - 1
    prev, nxt = (bi, jnp.maximum(si - 1, 0)), (bi, jnp.minimum(si + 1, ns - 1))

    def space_peer(d):
        return (bi, lax.rem(si + d, ns))

    def batch_peer(d):
        return (lax.rem(bi + d, nb), si)

    barrier = pltpu.get_barrier_semaphore()

    def hello(peer):
        pl.semaphore_signal(barrier, inc=1, device_id=peer, device_id_type=MESH)

    def every(numbers, act):
        if len(numbers) <= 8:
            for number in numbers:
                act(number)
        else:
            def step(index, carry):
                act(index + numbers[0])
                return carry
            lax.fori_loop(0, len(numbers), step, 0)

    loads = [pltpu.make_async_copy(dens.at[:, :, z], buf.at[z], load_sem.at[z]) for z in range(2)]
    pairs = ((w1_hbm, w1), (fold_hbm, fold), (w2_hbm, w2), (b1_hbm, b1), (b2_hbm, b2), (cot_hbm, cot))
    params = [pltpu.make_async_copy(src, dst, in_sem.at[n]) for n, (src, dst) in enumerate(pairs)]
    for copy in loads + params:
        copy.start()
    hello(space_peer(1))
    hello(space_peer(ns - 1))
    every(range(2, ns - 1), lambda d: hello(space_peer(d)))
    every(range(1, nb), lambda d: hello(batch_peer(d)))
    pl.semaphore_wait(barrier, ns - 1 + nb - 1)

    def remote(src, dst, send, recv, target):
        return pltpu.make_async_remote_copy(
            src_ref=src, dst_ref=dst, send_sem=send, recv_sem=recv, device_id=target, device_id_type=MESH
        )

    dens_copies = [
        [
            remote(buf.at[1 - side, b], buf.at[2 + side, b], dsend.at[b, side], drecv.at[b, side], (nxt, prev)[side])
            for side in range(2)
        ]
        for b in range(2)
    ]
    pool_copies = [
        [
            remote(
                pooled.at[piece // 2, :, pl.ds(piece % 2 * 512, 512)], halo2.at[piece // 2, side, :, pl.ds(piece % 2 * 512, 512)],
                psend.at[piece, side], precv.at[piece, side], (nxt, prev)[side],
            )
            for side in range(2)
        ]
        for piece in range(4)
    ]
    back_copies = [
        [
            remote(bsend.at[b, side], brecv.at[b, side], ksend.at[b, side], krecv.at[b, side], (nxt, prev)[side])
            for side in range(2)
        ]
        for b in range(2)
    ]
    gives, takes = (has_next, has_prev), (has_prev, has_next)

    odd = lax.rem(si, 2) == 1

    def start(copies):
        for turn in (odd, jnp.logical_not(odd)):
            pl.when(jnp.logical_and(gives[0], turn))(copies[0].start)
            pl.when(jnp.logical_and(gives[1], jnp.logical_not(turn)))(copies[1].start)

    def wait_in(copies):
        for side in range(2):
            pl.when(takes[side])(copies[side].wait_recv)

    def wait_out(copies):
        for side in range(2):
            pl.when(gives[side])(copies[side].wait_send)

    for copy in loads:
        copy.wait()
    for b in range(2):
        start(dens_copies[b])

    for side in range(2):
        def clear(side=side):
            buf[2 + side] = jnp.zeros(buf.shape[1:], BF16)
            for b in range(2):
                halo2[b, side] = jnp.zeros(halo2.shape[2:], BF16)
                brecv[b, side] = jnp.zeros(brecv.shape[2:], BF16)
        pl.when(jnp.logical_not(takes[side]))(clear)

    for copy in params:
        copy.wait()
    w1s[...] = jnp.zeros(w1s.shape, F32)
    w1s[:, 0:108] = w1[...].astype(F32)
    w1v = w1s[...].astype(BF16)
    for pos in range(8):
        wbig[pos * 32:(pos + 1) * 32, :] = dot(w1v, fold[:, pos * 256:(pos + 1) * 256]).astype(BF16)
    w2s[...] = jnp.zeros(w2s.shape, F32)
    w2s[:, 0:864] = w2[...].astype(F32)
    planes = (1, 0, 2)
    for j in range(3):
        for slot, i in enumerate(planes):
            lane = i * 288 + j * 96
            w2c[j * 64:(j + 1) * 64, slot * 96:(slot + 1) * 96] = w2s[:, lane:lane + 96].astype(BF16)
    for t4 in range(7):
        turned = w2s[:, t4 * 128:(t4 + 1) * 128].T
        for quarter in range(4):
            t = t4 * 4 + quarter
            if t < 27:
                i, j, k = t // 9, (t // 3) % 3, t % 3
                block = turned[quarter * 32:(quarter + 1) * 32, :]
                wb[j * 96 + i * 32:j * 96 + (i + 1) * 32, k * 64:(k + 1) * 64] = block.astype(BF16)
    bias1 = column_of(b1[...])
    bias1 = jnp.concatenate([bias1] * 8, axis=0)
    bias2 = column_of(b2[...])
    c9[...] = jnp.zeros(c9.shape, BF16)
    cb[...] = jnp.zeros(cb.shape, BF16)
    gs[...] = jnp.zeros(gs.shape, BF16)
    part[448:512, :] = jnp.zeros((64, 128), BF16)

    r, s = iota((256, 256), 0), iota((256, 256), 1)
    rows = (r & 192) + (r & 3) * 16 + ((r >> 3) & 7) * 2 + ((r >> 2) & 1)
    move_rows = (rows == s).astype(F32)[0:128, 0:128].astype(BF16)
    move_lanes = (r == (s & 127) * 2 + (s >> 7)).astype(F32).astype(BF16)

    def lay_out(pair, b):
        flat = buf[pair * 2:pair * 2 + 2, b].reshape(128, 256)
        moved = dot(move_rows, dot(flat, move_lanes).astype(BF16)).reshape(2, 8, 8, 256)
        gap = jnp.zeros((2, 1, 8, 256), F32)
        low = jnp.concatenate([gap, moved[:, :7]], axis=1)
        high = jnp.concatenate([moved[:, 1:], gap], axis=1)
        odd = iota(moved.shape, 2) >= 4
        beside = jnp.where(odd, low, high)
        for xg, field in enumerate((moved, beside)):
            even_y, odd_y = field[..., :128], field[..., 128:]
            for yg in range(2):
                halves = (even_y, odd_y) if yg == 0 else (after(even_y), before(odd_y))
                tile = jnp.concatenate(halves, axis=2).astype(BF16)
                for z in range(2):
                    row = ((pair * 2 + z) * 4 + xg * 2 + yg) * 16
                    for x in range(8):
                        lane = (b * 8 + x) * 128
                        cols1[row:row + 16, lane:lane + 128] = tile[z, x]

    for b in range(2):
        lay_out(0, b)

    def fill(target, row, height, b, field, flip):
        for x in range(8):
            lane = (b * 10 + 1 + x) * 128
            tile = field[:, x * 128:(x + 1) * 128]
            shifts = (before(tile), tile, after(tile))
            for k in range(3):
                piece = shifts[2 - k] if flip else shifts[k]
                target[row + k * height:row + (k + 1) * height, lane:lane + 128] = piece.astype(BF16)

    for b in range(2):
        wait_in(dens_copies[b])
        lay_out(1, b)
        for q in range(4):
            lane = b * 1024 + q * 256
            pre = dot(wbig[...], cols1[:, lane:lane + 256]) + bias1
            sig = sigmoid(pre)
            act = pre * sig
            d1[:, lane:lane + 256] = sig + act - act * sig
            total = act[0:32]
            for pos in range(1, 8):
                total = total + act[pos * 32:(pos + 1) * 32]
            pooled[b, :, q * 256:(q + 1) * 256] = (total * 0.125).astype(BF16)
            if q % 2 == 1:
                start(pool_copies[b * 2 + q // 2])
    for b in range(2):
        fill(c9, 0, 32, b, pooled[b].astype(F32), False)
        acc2[b] = dot(w2c[:, 0:96], c9[0:96, b * 1280:(b + 1) * 1280])
        trans[b] = cot[b].astype(F32)

    for b in range(2):
        wait_in(pool_copies[b * 2])
        wait_in(pool_copies[b * 2 + 1])
        for side in range(2):
            fill(c9, 96 + side * 96, 32, b, halo2[b, side].astype(F32), False)
        acc = acc2[b] + dot(w2c[:, 96:288], c9[96:288, b * 1280:(b + 1) * 1280])
        pre = acc[0:64, 0:1024] + acc[64:128, 128:1152] + acc[128:192, 256:1280] + bias2
        sig = sigmoid(pre)
        act = pre * sig
        slope = sig + act - act * sig
        grads = []
        for x in range(8):
            grads.append(trans[b, pl.ds(x, 64, stride=8), :] * slope[:, x * 128:(x + 1) * 128])
        grad = jnp.concatenate(grads, axis=1).astype(BF16)
        for j in range(3):
            lane = b * 1280 + j * 128
            gs[j * 64:(j + 1) * 64, lane:lane + 1024] = grad
        grad = grad.astype(F32)
        fill(cb, 0, 64, b, grad, True)
        acc = dot(wb[...], cb[:, b * 1280:(b + 1) * 1280])
        give = acc[0:96, 256:1280] + acc[96:192, 128:1152] + acc[192:288, 0:1024]
        bsend[b, 1] = give[0:32].astype(BF16)
        bsend[b, 0] = give[64:96].astype(BF16)
        start(back_copies[b])
        bown[:, b * 1024:(b + 1) * 1024] = give[32:64]
        acts[b] = act

    total = dot_nt(gs[...], c9[...])
    for j in range(3):
        for slot, i in enumerate(planes):
            lane = i * 288 + j * 96
            w2s[:, lane:lane + 96] = total[j * 64:(j + 1) * 64, slot * 96:(slot + 1) * 96]
    for t in range(7):
        part[t * 64:(t + 1) * 64, :] = w2s[:, t * 128:(t + 1) * 128].astype(BF16)

    size = 512 // ns

    def chunk(index):
        return pl.ds(pl.multiple_of(index * size, size), size)

    def rs_copy(d):
        return remote(part.at[chunk(lax.rem(si + d, ns))], rs_recv.at[d], rsend.at[d], rrecv.at[d], space_peer(d))

    def bx_copy(d):
        return remote(mine.at[0], bx_recv.at[bi], xsend.at[d], xrecv.at[d], batch_peer(d))

    def ag_copy(d):
        return remote(mine.at[1], full.at[chunk(si)], gsend.at[d], grecv.at[d], space_peer(d))

    def s1_copy(d):
        return remote(small, sm_recv.at[si], s1send.at[d], s1recv.at[d], space_peer(d))

    def s2_copy(d):
        return remote(sm_mid, sm_recv2.at[bi], s2send.at[d], s2recv.at[d], batch_peer(d))

    def each(count, make, act):
        every(range(1, count), lambda d: act(make(d)))

    def go(copy):
        copy.start()

    def arrive(copy):
        copy.wait_recv()

    def leave(copy):
        copy.wait_send()

    def in_order(terms, count):
        total = terms[0].astype(F32)
        for index in range(1, count):
            total = total + terms[index].astype(F32)
        return total

    live = -(-448 // size)

    def rs_go(d):
        pl.when(lax.rem(si + d, ns) < live)(rs_copy(d).start)

    def rs_leave(d):
        pl.when(lax.rem(si + d, ns) < live)(rs_copy(d).wait_send)

    def ag_arrive(d):
        pl.when(lax.rem(si + ns - d, ns) < live)(ag_copy(d).wait_recv)

    every(range(1, ns), rs_go)

    gb2 = jnp.sum(gs[64:128, :].astype(F32), axis=1, keepdims=True)
    for b in range(2):
        for x in range(8):
            trans[b, pl.ds(x, 64, stride=8), :] = acts[b, :, x * 128:(x + 1) * 128]
        feat[b] = trans[b].astype(BF16)

    gb1 = jnp.zeros((32, 256), F32)
    for b in range(2):
        wait_in(back_copies[b])
        for q in range(4):
            lane = b * 1024 + q * 256
            near = brecv[b, :, :, q * 256:(q + 1) * 256].astype(F32)
            back = (bown[:, lane:lane + 256] + near[0] + near[1]) * 0.125
            for pos in range(8):
                piece = (back * d1[pos * 32:(pos + 1) * 32, lane:lane + 256]).astype(BF16)
                gf[pos * 32:(pos + 1) * 32, lane:lane + 256] = piece
                gb1 = gb1 + piece.astype(F32)
        term = dot_nt(gf[:, b * 1024:(b + 1) * 1024], cols1[:, b * 1024:(b + 1) * 1024])
        if b == 0:
            held[...] = term
    gram = held[...] + term
    high = gram.astype(BF16)
    low = (gram - high.astype(F32)).astype(BF16)
    folded = jnp.zeros((64, 128), F32)
    for pos in range(8):
        both = jnp.concatenate([high[pos * 32:(pos + 1) * 32], low[pos * 32:(pos + 1) * 32]], axis=0)
        folded = folded + dot_nt(both, fold[:, pos * 256:(pos + 1) * 256])
    lane = iota((32, 128), 1)
    sums = folded[0:32] + folded[32:64]
    sums = jnp.where(lane == 108, jnp.sum(gb1, axis=1, keepdims=True), sums)
    sums = jnp.where(lane == 109, gb2[0:32], sums)
    small[...] = jnp.where(lane == 110, gb2[32:64], sums).astype(BF16)
    each(ns, s1_copy, go)

    @pl.when(si < live)
    def space_sum():
        each(ns, rs_copy, arrive)
        total = part[chunk(si), :].astype(F32)
        for d in range(1, ns):
            total = total + rs_recv[d].astype(F32)
        total = total.astype(BF16)
        mine[0] = total
        bx_recv[bi] = total
        each(nb, bx_copy, go)

    each(ns, s1_copy, arrive)
    sm_recv[si] = small[...]
    total = in_order(sm_recv, ns).astype(BF16)
    sm_mid[...] = total
    sm_recv2[bi] = total
    each(nb, s2_copy, go)

    @pl.when(si < live)
    def batch_sum():
        each(nb, bx_copy, arrive)
        total = in_order(bx_recv, nb).astype(BF16)
        mine[1] = total
        full[chunk(si), :] = total
        each(ns, ag_copy, go)

    for b in range(2):
        wait_out(dens_copies[b])
        wait_out(pool_copies[b * 2])
        wait_out(pool_copies[b * 2 + 1])
        wait_out(back_copies[b])
    every(range(1, ns), rs_leave)
    each(ns, s1_copy, leave)
    each(nb, s2_copy, arrive)
    total = in_order(sm_recv2, nb)
    gw1_out[...] = total[:, 0:108]
    gb1_out[...] = row_of(total[:, 108:109])
    gb2_out[...] = row_of(jnp.concatenate([total[:, 109:110], total[:, 110:111]], axis=0))

    each(nb, s2_copy, leave)
    every(range(1, ns), ag_arrive)
    for t in range(7):
        width = min(128, 864 - t * 128)
        gw2_out[:, t * 128:t * 128 + width] = full[t * 64:(t + 1) * 64, 0:width].astype(F32)

    @pl.when(si < live)
    def done():
        each(nb, bx_copy, leave)
        each(ns, ag_copy, leave)


def hand_out(*refs):
    held, results, sems = refs[0:5], refs[5:10], refs[10]
    outward = [pltpu.make_async_copy(held[n], results[n], sems.at[n]) for n in range(5)]
    for copy in outward:
        copy.start()
    for copy in outward:
        copy.wait()


def body(nb, ns, density, w_first, b_first, w_second, b_second, cotangent):
    vmem = pl.BlockSpec(memory_space=pltpu.VMEM)
    hbm = pl.BlockSpec(memory_space=pltpu.HBM)
    dma = pltpu.SemaphoreType.DMA
    size = 512 // ns
    shapes = (
        jax.ShapeDtypeStruct((2, 512, 128), BF16),
        jax.ShapeDtypeStruct((32, 108), F32),
        jax.ShapeDtypeStruct((1, 32), F32),
        jax.ShapeDtypeStruct((64, 864), F32),
        jax.ShapeDtypeStruct((1, 64), F32),
    )
    held = pl.pallas_call(
        functools.partial(kernel, nb, ns),
        out_shape=tuple(pltpu.VMEM(one.shape, one.dtype) for one in shapes),
        in_specs=[hbm] * 7,
        out_specs=(vmem,) * 5,
        scratch_shapes=[
            pltpu.VMEM((32, 108), BF16),
            pltpu.VMEM((1, 32), F32),
            pltpu.VMEM((64, 864), BF16),
            pltpu.VMEM((1, 64), F32),
            pltpu.VMEM((2, 512, 128), BF16),
            pltpu.VMEM((128, 2048), BF16),
            pltpu.VMEM((4, 2, 4, 16, 256), BF16),
            pltpu.VMEM((256, 2048), BF16),
            pltpu.VMEM((256, 256), BF16),
            pltpu.VMEM((256, 2048), F32),
            pltpu.VMEM((32, 128), F32),
            pltpu.VMEM((64, 896), F32),
            pltpu.VMEM((192, 288), BF16),
            pltpu.VMEM((288, 192), BF16),
            pltpu.VMEM((2, 32, 1024), BF16),
            pltpu.VMEM((2, 2, 32, 1024), BF16),
            pltpu.VMEM((288, 2560), BF16),
            pltpu.VMEM((2, 192, 1280), F32),
            pltpu.VMEM((2, 512, 128), F32),
            pltpu.VMEM((2, 64, 1024), F32),
            pltpu.VMEM((256, 256), F32),
            pltpu.VMEM((192, 2560), BF16),
            pltpu.VMEM((192, 2560), BF16),
            pltpu.VMEM((2, 2, 32, 1024), BF16),
            pltpu.VMEM((2, 2, 32, 1024), BF16),
            pltpu.VMEM((32, 2048), F32),
            pltpu.VMEM((256, 2048), BF16),
            pltpu.VMEM((512, 128), BF16),
            pltpu.VMEM((ns, size, 128), BF16),
            pltpu.VMEM((2, size, 128), BF16),
            pltpu.VMEM((nb, size, 128), BF16),
            pltpu.VMEM((512, 128), BF16),
            pltpu.VMEM((32, 128), BF16),
            pltpu.VMEM((ns, 32, 128), BF16),
            pltpu.VMEM((32, 128), BF16),
            pltpu.VMEM((nb, 32, 128), BF16),
            dma((2,)), dma((6,)), dma((2, 2)), dma((2, 2)),
            dma((4, 2)), dma((4, 2)), dma((2, 2)), dma((2, 2)),
            dma((ns,)), dma((ns,)), dma((nb,)), dma((nb,)), dma((ns,)), dma((ns,)),
            dma((ns,)), dma((ns,)), dma((nb,)), dma((nb,)),
        ],
        compiler_params=pltpu.CompilerParams(
            collective_id=0, has_side_effects=True, vmem_limit_bytes=40 * 1024 * 1024
        ),
        cost_estimate=pl.CostEstimate(flops=1 << 30, bytes_accessed=1 << 21, transcendentals=1 << 20),
    )(*[
        pltpu.with_memory_space_constraint(one, pltpu.HBM)
        for one in (
            density, w_first, b_first.reshape(1, 32), w_second, b_second.reshape(1, 64), cotangent.reshape(2, 512, 128),
            jnp.asarray(fold_matrix(), BF16),
        )
    ])
    feat, gw1, gb1, gw2, gb2 = pl.pallas_call(
        hand_out,
        out_shape=shapes,
        in_specs=[vmem] * 5,
        out_specs=(hbm,) * 5,
        scratch_shapes=[dma((5,))],
        compiler_params=pltpu.CompilerParams(vmem_limit_bytes=8 * 1024 * 1024),
    )(*held)
    return feat.reshape(cotangent.shape), gw1, gb1.reshape(32), gw2, gb2.reshape(64)


def solution(mesh):
    data = P("batch", None, "space", None, None)
    return jax.shard_map(
        functools.partial(body, mesh.shape["batch"], mesh.shape["space"]),
        mesh=mesh,
        in_specs=(data, P(), P(), P(), P(), data),
        out_specs=(data, P(), P(), P(), P()),
        check_vma=False,
    )
```

```python
import functools

import jax
import jax.numpy as jnp
import numpy as np
from jax import lax
from jax.experimental import pallas as pl
from jax.experimental.pallas import tpu as pltpu
from jax.sharding import PartitionSpec as P

F32 = jnp.float32
BF16 = jnp.bfloat16
MESH = pl.DeviceIdType.MESH
NT = (((1,), (1,)), ((), ()))


def fold_matrix():
    fold = np.zeros((128, 8, 256), np.float32)

    def coordinate(group, parity):
        return 1 + parity if group == 0 else (0 if parity == 1 else 3)

    planes = (1, 2, 0, 3)
    for row in range(256):
        zi, xg, yg = row >> 6, (row >> 5) & 1, (row >> 4) & 1
        yp, xp, c = (row >> 3) & 1, (row >> 2) & 1, row & 3
        zz, xx, yy = planes[zi], coordinate(xg, xp), coordinate(yg, yp)
        for pos in range(8):
            i, j, k = zz - (pos >> 2), xx - ((pos >> 1) & 1), yy - (pos & 1)
            if 0 <= i < 3 and 0 <= j < 3 and 0 <= k < 3:
                fold[((i * 3 + j) * 3 + k) * 4 + c, pos, row] = 1
    return fold.reshape(128, 2048)


def iota(shape, axis):
    return lax.broadcasted_iota(jnp.int32, shape, axis)


def sigmoid(value):
    return 0.5 + 0.5 * jnp.tanh(0.5 * value)


def column_of(row):
    size = row.shape[1]
    eye = iota((size, size), 0) == iota((size, size), 1)
    return jnp.sum(jnp.where(eye, row, 0.0), axis=1, keepdims=True)


def row_of(column):
    size = column.shape[0]
    eye = iota((size, size), 0) == iota((size, size), 1)
    return jnp.sum(jnp.where(eye, column, 0.0), axis=0, keepdims=True)


def dot(a, b):
    return jnp.dot(a, b, preferred_element_type=F32)


def dot_nt(a, b):
    return lax.dot_general(a, b, NT, preferred_element_type=F32)


def before(tile):
    axis = tile.ndim - 1
    return jnp.where(iota(tile.shape, axis) == 0, 0.0, pltpu.roll(tile, 1, axis))


def after(tile):
    axis = tile.ndim - 1
    return jnp.where(iota(tile.shape, axis) == 127, 0.0, pltpu.roll(tile, 127, axis))


def kernel(
    nb, ns,
    dens, w1_hbm, b1_hbm, w2_hbm, b2_hbm, cot_hbm, fold_hbm,
    feat, gw1_out, gb1_out, gw2_out, gb2_out,
    w1, b1, w2, b2, cot, fold, buf, cols1, wbig, d1, w1s, w2s, w2c, wb, pooled, halo2, c9, acc2, trans, acts, held, gs, cb, bsend, brecv, bown, gf,
    part, rs_recv, mine, bx_recv, full, small, sm_recv, sm_mid, sm_recv2,
    load_sem, in_sem, dsend, drecv, psend, precv, ksend, krecv, rsend, rrecv, xsend, xrecv, gsend, grecv,
    s1send, s1recv, s2send, s2recv,
):
    bi = lax.axis_index("batch")
    si = lax.axis_index("space")
    has_prev, has_next = si > 0, si < ns - 1
    prev, nxt = (bi, jnp.maximum(si - 1, 0)), (bi, jnp.minimum(si + 1, ns - 1))

    def space_peer(d):
        return (bi, lax.rem(si + d, ns))

    def batch_peer(d):
        return (lax.rem(bi + d, nb), si)

    barrier = pltpu.get_barrier_semaphore()

    def hello(peer):
        pl.semaphore_signal(barrier, inc=1, device_id=peer, device_id_type=MESH)

    def every(numbers, act):
        if len(numbers) <= 8:
            for number in numbers:
                act(number)
        else:
            def step(index, carry):
                act(index + numbers[0])
                return carry
            lax.fori_loop(0, len(numbers), step, 0)

    loads = [pltpu.make_async_copy(dens.at[:, :, z], buf.at[z], load_sem.at[z]) for z in range(2)]
    pairs = ((w1_hbm, w1), (fold_hbm, fold), (w2_hbm, w2), (b1_hbm, b1), (b2_hbm, b2), (cot_hbm, cot))
    params = [pltpu.make_async_copy(src, dst, in_sem.at[n]) for n, (src, dst) in enumerate(pairs)]
    for copy in loads + params:
        copy.start()
    hello(space_peer(1))
    hello(space_peer(ns - 1))
    every(range(2, ns - 1), lambda d: hello(space_peer(d)))
    every(range(1, nb), lambda d: hello(batch_peer(d)))
    pl.semaphore_wait(barrier, ns - 1 + nb - 1)

    def remote(src, dst, send, recv, target):
        return pltpu.make_async_remote_copy(
            src_ref=src, dst_ref=dst, send_sem=send, recv_sem=recv, device_id=target, device_id_type=MESH
        )

    dens_copies = [
        [
            remote(buf.at[1 - side, b], buf.at[2 + side, b], dsend.at[b, side], drecv.at[b, side], (nxt, prev)[side])
            for side in range(2)
        ]
        for b in range(2)
    ]
    pool_copies = [
        [
            remote(
                pooled.at[piece // 2, :, pl.ds(piece % 2 * 512, 512)], halo2.at[piece // 2, side, :, pl.ds(piece % 2 * 512, 512)],
                psend.at[piece, side], precv.at[piece, side], (nxt, prev)[side],
            )
            for side in range(2)
        ]
        for piece in range(4)
    ]
    back_copies = [
        [
            remote(bsend.at[b, side], brecv.at[b, side], ksend.at[b, side], krecv.at[b, side], (nxt, prev)[side])
            for side in range(2)
        ]
        for b in range(2)
    ]
    gives, takes = (has_next, has_prev), (has_prev, has_next)

    odd = lax.rem(si, 2) == 1

    def start(copies):
        for turn in (odd, jnp.logical_not(odd)):
            pl.when(jnp.logical_and(gives[0], turn))(copies[0].start)
            pl.when(jnp.logical_and(gives[1], jnp.logical_not(turn)))(copies[1].start)

    def wait_in(copies):
        for side in range(2):
            pl.when(takes[side])(copies[side].wait_recv)

    def wait_out(copies):
        for side in range(2):
            pl.when(gives[side])(copies[side].wait_send)

    for copy in loads:
        copy.wait()
    for b in range(2):
        start(dens_copies[b])

    for side in range(2):
        def clear(side=side):
            buf[2 + side] = jnp.zeros(buf.shape[1:], BF16)
            for b in range(2):
                halo2[b, side] = jnp.zeros(halo2.shape[2:], BF16)
                brecv[b, side] = jnp.zeros(brecv.shape[2:], BF16)
        pl.when(jnp.logical_not(takes[side]))(clear)

    for copy in params:
        copy.wait()
    w1s[...] = jnp.zeros(w1s.shape, F32)
    w1s[:, 0:108] = w1[...].astype(F32)
    w1v = w1s[...].astype(BF16)
    for pos in range(8):
        wbig[pos * 32:(pos + 1) * 32, :] = dot(w1v, fold[:, pos * 256:(pos + 1) * 256]).astype(BF16)
    w2s[...] = jnp.zeros(w2s.shape, F32)
    w2s[:, 0:864] = w2[...].astype(F32)
    planes = (1, 0, 2)
    for j in range(3):
        for slot, i in enumerate(planes):
            lane = i * 288 + j * 96
            w2c[j * 64:(j + 1) * 64, slot * 96:(slot + 1) * 96] = w2s[:, lane:lane + 96].astype(BF16)
    for t4 in range(7):
        turned = w2s[:, t4 * 128:(t4 + 1) * 128].T
        for quarter in range(4):
            t = t4 * 4 + quarter
            if t < 27:
                i, j, k = t // 9, (t // 3) % 3, t % 3
                block = turned[quarter * 32:(quarter + 1) * 32, :]
                wb[j * 96 + i * 32:j * 96 + (i + 1) * 32, k * 64:(k + 1) * 64] = block.astype(BF16)
    bias1 = column_of(b1[...])
    bias1 = jnp.concatenate([bias1] * 8, axis=0)
    bias2 = column_of(b2[...])
    c9[...] = jnp.zeros(c9.shape, BF16)
    cb[...] = jnp.zeros(cb.shape, BF16)
    gs[...] = jnp.zeros(gs.shape, BF16)
    part[448:512, :] = jnp.zeros((64, 128), BF16)

    r, s = iota((256, 256), 0), iota((256, 256), 1)
    rows = (r & 192) + (r & 3) * 16 + ((r >> 3) & 7) * 2 + ((r >> 2) & 1)
    move_rows = (rows == s).astype(F32)[0:128, 0:128].astype(BF16)
    move_lanes = (r == (s & 127) * 2 + (s >> 7)).astype(F32).astype(BF16)

    def lay_out(pair, b):
        flat = buf[pair * 2:pair * 2 + 2, b].reshape(128, 256)
        moved = dot(move_rows, dot(flat, move_lanes).astype(BF16)).reshape(2, 8, 8, 256)
        gap = jnp.zeros((2, 1, 8, 256), F32)
        low = jnp.concatenate([gap, moved[:, :7]], axis=1)
        high = jnp.concatenate([moved[:, 1:], gap], axis=1)
        odd = iota(moved.shape, 2) >= 4
        beside = jnp.where(odd, low, high)
        for xg, field in enumerate((moved, beside)):
            even_y, odd_y = field[..., :128], field[..., 128:]
            for yg in range(2):
                halves = (even_y, odd_y) if yg == 0 else (after(even_y), before(odd_y))
                tile = jnp.concatenate(halves, axis=2).astype(BF16)
                for z in range(2):
                    row = ((pair * 2 + z) * 4 + xg * 2 + yg) * 16
                    for x in range(8):
                        lane = (b * 8 + x) * 128
                        cols1[row:row + 16, lane:lane + 128] = tile[z, x]

    for b in range(2):
        lay_out(0, b)

    def fill(target, row, height, b, field, flip, cells=range(8)):
        for x in cells:
            lane = (b * 10 + 1 + x) * 128
            tile = field[:, x * 128:(x + 1) * 128].astype(F32)
            shifts = (before(tile), tile, after(tile))
            for k in range(3):
                piece = shifts[2 - k] if flip else shifts[k]
                target[row + k * height:row + (k + 1) * height, lane:lane + 128] = piece.astype(BF16)

    for b in range(2):
        wait_in(dens_copies[b])
        lay_out(1, b)
        for q in range(4):
            lane = b * 1024 + q * 256
            pre = dot(wbig[...], cols1[:, lane:lane + 256]) + bias1
            sig = sigmoid(pre)
            act = pre * sig
            d1[:, lane:lane + 256] = sig + act - act * sig
            total = act[0:32]
            for pos in range(1, 8):
                total = total + act[pos * 32:(pos + 1) * 32]
            pooled[b, :, q * 256:(q + 1) * 256] = (total * 0.125).astype(BF16)
            if q % 2 == 1:
                start(pool_copies[b * 2 + q // 2])
    for b in range(2):
        fill(c9, 0, 32, b, pooled[b].astype(F32), False)
        acc2[b] = dot(w2c[:, 0:96], c9[0:96, b * 1280:(b + 1) * 1280])
        trans[b] = cot[b].astype(F32)

    for b in range(2):
        for half in range(2):
            wait_in(pool_copies[b * 2 + half])
            for side in range(2):
                fill(c9, 96 + side * 96, 32, b, halo2.at[b, side], False, range(half * 4, half * 4 + 4))
        acc = acc2[b] + dot(w2c[:, 96:288], c9[96:288, b * 1280:(b + 1) * 1280])
        pre = acc[0:64, 0:1024] + acc[64:128, 128:1152] + acc[128:192, 256:1280] + bias2
        sig = sigmoid(pre)
        act = pre * sig
        slope = sig + act - act * sig
        grads = []
        for x in range(8):
            grads.append(trans[b, pl.ds(x, 64, stride=8), :] * slope[:, x * 128:(x + 1) * 128])
        grad = jnp.concatenate(grads, axis=1).astype(BF16)
        for j in range(3):
            lane = b * 1280 + j * 128
            gs[j * 64:(j + 1) * 64, lane:lane + 1024] = grad
        grad = grad.astype(F32)
        fill(cb, 0, 64, b, grad, True)
        acc = dot(wb[...], cb[:, b * 1280:(b + 1) * 1280])
        give = acc[0:96, 256:1280] + acc[96:192, 128:1152] + acc[192:288, 0:1024]
        bsend[b, 1] = give[0:32].astype(BF16)
        bsend[b, 0] = give[64:96].astype(BF16)
        start(back_copies[b])
        bown[:, b * 1024:(b + 1) * 1024] = give[32:64]
        acts[b] = act

    total = dot_nt(gs[...], c9[...])
    for j in range(3):
        for slot, i in enumerate(planes):
            lane = i * 288 + j * 96
            w2s[:, lane:lane + 96] = total[j * 64:(j + 1) * 64, slot * 96:(slot + 1) * 96]
    for t in range(7):
        part[t * 64:(t + 1) * 64, :] = w2s[:, t * 128:(t + 1) * 128].astype(BF16)

    size = 512 // ns

    def chunk(index):
        return pl.ds(pl.multiple_of(index * size, size), size)

    def rs_copy(d):
        return remote(part.at[chunk(lax.rem(si + d, ns))], rs_recv.at[d], rsend.at[d], rrecv.at[d], space_peer(d))

    def bx_copy(d):
        return remote(mine.at[0], bx_recv.at[bi], xsend.at[d], xrecv.at[d], batch_peer(d))

    def ag_copy(d):
        return remote(mine.at[1], full.at[chunk(si)], gsend.at[d], grecv.at[d], space_peer(d))

    def s1_copy(d):
        return remote(small, sm_recv.at[si], s1send.at[d], s1recv.at[d], space_peer(d))

    def s2_copy(d):
        return remote(sm_mid, sm_recv2.at[bi], s2send.at[d], s2recv.at[d], batch_peer(d))

    def each(count, make, act):
        every(range(1, count), lambda d: act(make(d)))

    def go(copy):
        copy.start()

    def arrive(copy):
        copy.wait_recv()

    def leave(copy):
        copy.wait_send()

    def in_order(terms, count):
        total = terms[0].astype(F32)
        for index in range(1, count):
            total = total + terms[index].astype(F32)
        return total

    live = -(-448 // size)

    def rs_go(d):
        pl.when(lax.rem(si + d, ns) < live)(rs_copy(d).start)

    def rs_leave(d):
        pl.when(lax.rem(si + d, ns) < live)(rs_copy(d).wait_send)

    def ag_arrive(d):
        pl.when(lax.rem(si + ns - d, ns) < live)(ag_copy(d).wait_recv)

    every(range(1, ns), rs_go)

    gb2 = jnp.sum(gs[64:128, :].astype(F32), axis=1, keepdims=True)
    for b in range(2):
        for x in range(8):
            trans[b, pl.ds(x, 64, stride=8), :] = acts[b, :, x * 128:(x + 1) * 128]
        feat[b] = trans[b].astype(BF16)

    gb1 = jnp.zeros((32, 256), F32)
    for b in range(2):
        wait_in(back_copies[b])
        for q in range(4):
            lane = b * 1024 + q * 256
            near = brecv[b, :, :, q * 256:(q + 1) * 256].astype(F32)
            back = (bown[:, lane:lane + 256] + near[0] + near[1]) * 0.125
            for pos in range(8):
                piece = (back * d1[pos * 32:(pos + 1) * 32, lane:lane + 256]).astype(BF16)
                gf[pos * 32:(pos + 1) * 32, lane:lane + 256] = piece
                gb1 = gb1 + piece.astype(F32)
        term = dot_nt(gf[:, b * 1024:(b + 1) * 1024], cols1[:, b * 1024:(b + 1) * 1024])
        if b == 0:
            held[...] = term
    gram = held[...] + term
    high = gram.astype(BF16)
    low = (gram - high.astype(F32)).astype(BF16)
    folded = jnp.zeros((64, 128), F32)
    for pos in range(8):
        both = jnp.concatenate([high[pos * 32:(pos + 1) * 32], low[pos * 32:(pos + 1) * 32]], axis=0)
        folded = folded + dot_nt(both, fold[:, pos * 256:(pos + 1) * 256])
    lane = iota((32, 128), 1)
    sums = folded[0:32] + folded[32:64]
    sums = jnp.where(lane == 108, jnp.sum(gb1, axis=1, keepdims=True), sums)
    sums = jnp.where(lane == 109, gb2[0:32], sums)
    small[...] = jnp.where(lane == 110, gb2[32:64], sums).astype(BF16)
    each(ns, s1_copy, go)

    @pl.when(si < live)
    def space_sum():
        each(ns, rs_copy, arrive)
        total = part[chunk(si), :].astype(F32)
        for d in range(1, ns):
            total = total + rs_recv[d].astype(F32)
        total = total.astype(BF16)
        mine[0] = total
        bx_recv[bi] = total
        each(nb, bx_copy, go)

    each(ns, s1_copy, arrive)
    sm_recv[si] = small[...]
    total = in_order(sm_recv, ns).astype(BF16)
    sm_mid[...] = total
    sm_recv2[bi] = total
    each(nb, s2_copy, go)

    @pl.when(si < live)
    def batch_sum():
        each(nb, bx_copy, arrive)
        total = in_order(bx_recv, nb).astype(BF16)
        mine[1] = total
        full[chunk(si), :] = total
        each(ns, ag_copy, go)

    for b in range(2):
        wait_out(dens_copies[b])
        wait_out(pool_copies[b * 2])
        wait_out(pool_copies[b * 2 + 1])
        wait_out(back_copies[b])
    every(range(1, ns), rs_leave)
    each(ns, s1_copy, leave)
    each(nb, s2_copy, arrive)
    total = in_order(sm_recv2, nb)
    gw1_out[...] = total[:, 0:108]
    gb1_out[...] = row_of(total[:, 108:109])
    gb2_out[...] = row_of(jnp.concatenate([total[:, 109:110], total[:, 110:111]], axis=0))

    each(nb, s2_copy, leave)
    every(range(1, ns), ag_arrive)
    for t in range(7):
        width = min(128, 864 - t * 128)
        gw2_out[:, t * 128:t * 128 + width] = full[t * 64:(t + 1) * 64, 0:width].astype(F32)

    @pl.when(si < live)
    def done():
        each(nb, bx_copy, leave)
        each(ns, ag_copy, leave)


def hand_out(*refs):
    held, results, sems = refs[0:5], refs[5:10], refs[10]
    outward = [pltpu.make_async_copy(held[n], results[n], sems.at[n]) for n in range(5)]
    for copy in outward:
        copy.start()
    for copy in outward:
        copy.wait()


def body(nb, ns, density, w_first, b_first, w_second, b_second, cotangent):
    vmem = pl.BlockSpec(memory_space=pltpu.VMEM)
    hbm = pl.BlockSpec(memory_space=pltpu.HBM)
    dma = pltpu.SemaphoreType.DMA
    size = 512 // ns
    shapes = (
        jax.ShapeDtypeStruct((2, 512, 128), BF16),
        jax.ShapeDtypeStruct((32, 108), F32),
        jax.ShapeDtypeStruct((1, 32), F32),
        jax.ShapeDtypeStruct((64, 864), F32),
        jax.ShapeDtypeStruct((1, 64), F32),
    )
    held = pl.pallas_call(
        functools.partial(kernel, nb, ns),
        out_shape=tuple(pltpu.VMEM(one.shape, one.dtype) for one in shapes),
        in_specs=[hbm] * 7,
        out_specs=(vmem,) * 5,
        scratch_shapes=[
            pltpu.VMEM((32, 108), BF16),
            pltpu.VMEM((1, 32), F32),
            pltpu.VMEM((64, 864), BF16),
            pltpu.VMEM((1, 64), F32),
            pltpu.VMEM((2, 512, 128), BF16),
            pltpu.VMEM((128, 2048), BF16),
            pltpu.VMEM((4, 2, 4, 16, 256), BF16),
            pltpu.VMEM((256, 2048), BF16),
            pltpu.VMEM((256, 256), BF16),
            pltpu.VMEM((256, 2048), F32),
            pltpu.VMEM((32, 128), F32),
            pltpu.VMEM((64, 896), F32),
            pltpu.VMEM((192, 288), BF16),
            pltpu.VMEM((288, 192), BF16),
            pltpu.VMEM((2, 32, 1024), BF16),
            pltpu.VMEM((2, 2, 32, 1024), BF16),
            pltpu.VMEM((288, 2560), BF16),
            pltpu.VMEM((2, 192, 1280), F32),
            pltpu.VMEM((2, 512, 128), F32),
            pltpu.VMEM((2, 64, 1024), F32),
            pltpu.VMEM((256, 256), F32),
            pltpu.VMEM((192, 2560), BF16),
            pltpu.VMEM((192, 2560), BF16),
            pltpu.VMEM((2, 2, 32, 1024), BF16),
            pltpu.VMEM((2, 2, 32, 1024), BF16),
            pltpu.VMEM((32, 2048), F32),
            pltpu.VMEM((256, 2048), BF16),
            pltpu.VMEM((512, 128), BF16),
            pltpu.VMEM((ns, size, 128), BF16),
            pltpu.VMEM((2, size, 128), BF16),
            pltpu.VMEM((nb, size, 128), BF16),
            pltpu.VMEM((512, 128), BF16),
            pltpu.VMEM((32, 128), BF16),
            pltpu.VMEM((ns, 32, 128), BF16),
            pltpu.VMEM((32, 128), BF16),
            pltpu.VMEM((nb, 32, 128), BF16),
            dma((2,)), dma((6,)), dma((2, 2)), dma((2, 2)),
            dma((4, 2)), dma((4, 2)), dma((2, 2)), dma((2, 2)),
            dma((ns,)), dma((ns,)), dma((nb,)), dma((nb,)), dma((ns,)), dma((ns,)),
            dma((ns,)), dma((ns,)), dma((nb,)), dma((nb,)),
        ],
        compiler_params=pltpu.CompilerParams(
            collective_id=0, has_side_effects=True, vmem_limit_bytes=40 * 1024 * 1024
        ),
        cost_estimate=pl.CostEstimate(flops=1 << 30, bytes_accessed=1 << 21, transcendentals=1 << 20),
    )(*[
        pltpu.with_memory_space_constraint(one, pltpu.HBM)
        for one in (
            density, w_first, b_first.reshape(1, 32), w_second, b_second.reshape(1, 64), cotangent.reshape(2, 512, 128),
            jnp.asarray(fold_matrix(), BF16),
        )
    ])
    feat, gw1, gb1, gw2, gb2 = pl.pallas_call(
        hand_out,
        out_shape=shapes,
        in_specs=[vmem] * 5,
        out_specs=(hbm,) * 5,
        scratch_shapes=[dma((5,))],
        compiler_params=pltpu.CompilerParams(vmem_limit_bytes=8 * 1024 * 1024),
    )(*held)
    return feat.reshape(cotangent.shape), gw1, gb1.reshape(32), gw2, gb2.reshape(64)


def solution(mesh):
    data = P("batch", None, "space", None, None)
    return jax.shard_map(
        functools.partial(body, mesh.shape["batch"], mesh.shape["space"]),
        mesh=mesh,
        in_specs=(data, P(), P(), P(), P(), data),
        out_specs=(data, P(), P(), P(), P()),
        check_vma=False,
    )
```

```python
import functools

import jax
import jax.numpy as jnp
import numpy as np
from jax import lax
from jax.experimental import pallas as pl
from jax.experimental.pallas import tpu as pltpu
from jax.sharding import PartitionSpec as P

F32 = jnp.float32
BF16 = jnp.bfloat16
MESH = pl.DeviceIdType.MESH
NT = (((1,), (1,)), ((), ()))


def fold_matrix():
    fold = np.zeros((128, 8, 256), np.float32)

    def coordinate(group, parity):
        return 1 + parity if group == 0 else (0 if parity == 1 else 3)

    planes = (1, 2, 0, 3)
    for row in range(256):
        zi, xg, yg = row >> 6, (row >> 5) & 1, (row >> 4) & 1
        yp, xp, c = (row >> 3) & 1, (row >> 2) & 1, row & 3
        zz, xx, yy = planes[zi], coordinate(xg, xp), coordinate(yg, yp)
        for pos in range(8):
            i, j, k = zz - (pos >> 2), xx - ((pos >> 1) & 1), yy - (pos & 1)
            if 0 <= i < 3 and 0 <= j < 3 and 0 <= k < 3:
                fold[((i * 3 + j) * 3 + k) * 4 + c, pos, row] = 1
    return fold.reshape(128, 2048)


def iota(shape, axis):
    return lax.broadcasted_iota(jnp.int32, shape, axis)


def sigmoid(value):
    return 0.5 + 0.5 * jnp.tanh(0.5 * value)


def column_of(row):
    size = row.shape[1]
    eye = iota((size, size), 0) == iota((size, size), 1)
    return jnp.sum(jnp.where(eye, row, 0.0), axis=1, keepdims=True)


def row_of(column):
    size = column.shape[0]
    eye = iota((size, size), 0) == iota((size, size), 1)
    return jnp.sum(jnp.where(eye, column, 0.0), axis=0, keepdims=True)


def dot(a, b):
    return jnp.dot(a, b, preferred_element_type=F32)


def dot_nt(a, b):
    return lax.dot_general(a, b, NT, preferred_element_type=F32)


def before(tile):
    axis = tile.ndim - 1
    return jnp.where(iota(tile.shape, axis) == 0, 0.0, pltpu.roll(tile, 1, axis))


def after(tile):
    axis = tile.ndim - 1
    return jnp.where(iota(tile.shape, axis) == 127, 0.0, pltpu.roll(tile, 127, axis))


def kernel(
    nb, ns,
    dens, w1_hbm, b1_hbm, w2_hbm, b2_hbm, cot_hbm, fold_hbm,
    feat, gw1_out, gb1_out, gw2_out, gb2_out,
    w1, b1, w2, b2, cot, fold, buf, cols1, wbig, d1, w1s, w2s, w2c, wb, pooled, halo2, c9, acc2, trans, acts, held, gs, cb, bsend, brecv, bown, gf,
    part, rs_recv, mine, bx_recv, full, small, sm_recv, sm_mid, sm_recv2,
    load_sem, in_sem, dsend, drecv, psend, precv, ksend, krecv, rsend, rrecv, xsend, xrecv, gsend, grecv,
    s1send, s1recv, s2send, s2recv,
):
    bi = lax.axis_index("batch")
    si = lax.axis_index("space")
    has_prev, has_next = si > 0, si < ns - 1
    prev, nxt = (bi, jnp.maximum(si - 1, 0)), (bi, jnp.minimum(si + 1, ns - 1))

    def space_peer(d):
        return (bi, lax.rem(si + d, ns))

    def batch_peer(d):
        return (lax.rem(bi + d, nb), si)

    barrier = pltpu.get_barrier_semaphore()

    def hello(peer):
        pl.semaphore_signal(barrier, inc=1, device_id=peer, device_id_type=MESH)

    def every(numbers, act):
        if len(numbers) <= 8:
            for number in numbers:
                act(number)
        else:
            def step(index, carry):
                act(index + numbers[0])
                return carry
            lax.fori_loop(0, len(numbers), step, 0)

    loads = [pltpu.make_async_copy(dens.at[:, :, z], buf.at[z], load_sem.at[z]) for z in range(2)]
    pairs = ((w1_hbm, w1), (fold_hbm, fold), (w2_hbm, w2), (b1_hbm, b1), (b2_hbm, b2), (cot_hbm, cot))
    params = [pltpu.make_async_copy(src, dst, in_sem.at[n]) for n, (src, dst) in enumerate(pairs)]
    for copy in loads + params:
        copy.start()
    hello(space_peer(1))
    hello(space_peer(ns - 1))
    every(range(2, ns - 1), lambda d: hello(space_peer(d)))
    every(range(1, nb), lambda d: hello(batch_peer(d)))
    pl.semaphore_wait(barrier, ns - 1 + nb - 1)

    def remote(src, dst, send, recv, target):
        return pltpu.make_async_remote_copy(
            src_ref=src, dst_ref=dst, send_sem=send, recv_sem=recv, device_id=target, device_id_type=MESH
        )

    dens_copies = [
        [
            remote(buf.at[1 - side, b], buf.at[2 + side, b], dsend.at[b, side], drecv.at[b, side], (nxt, prev)[side])
            for side in range(2)
        ]
        for b in range(2)
    ]
    pool_copies = [
        [
            remote(
                pooled.at[piece // 2, :, pl.ds(piece % 2 * 512, 512)], halo2.at[piece // 2, side, :, pl.ds(piece % 2 * 512, 512)],
                psend.at[piece, side], precv.at[piece, side], (nxt, prev)[side],
            )
            for side in range(2)
        ]
        for piece in range(4)
    ]
    back_copies = [
        [
            remote(bsend.at[b, side], brecv.at[b, side], ksend.at[b, side], krecv.at[b, side], (nxt, prev)[side])
            for side in range(2)
        ]
        for b in range(2)
    ]
    gives, takes = (has_next, has_prev), (has_prev, has_next)

    odd = lax.rem(si, 2) == 1

    def start(copies):
        for turn in (odd, jnp.logical_not(odd)):
            pl.when(jnp.logical_and(gives[0], turn))(copies[0].start)
            pl.when(jnp.logical_and(gives[1], jnp.logical_not(turn)))(copies[1].start)

    def wait_in(copies):
        for side in range(2):
            pl.when(takes[side])(copies[side].wait_recv)

    def wait_out(copies):
        for side in range(2):
            pl.when(gives[side])(copies[side].wait_send)

    for copy in loads:
        copy.wait()
    for b in range(2):
        start(dens_copies[b])

    for side in range(2):
        def clear(side=side):
            buf[2 + side] = jnp.zeros(buf.shape[1:], BF16)
            for b in range(2):
                halo2[b, side] = jnp.zeros(halo2.shape[2:], BF16)
                brecv[b, side] = jnp.zeros(brecv.shape[2:], BF16)
        pl.when(jnp.logical_not(takes[side]))(clear)

    for copy in params:
        copy.wait()
    w1s[...] = jnp.zeros(w1s.shape, F32)
    w1s[:, 0:108] = w1[...].astype(F32)
    w1v = w1s[...].astype(BF16)
    for pos in range(8):
        wbig[pos * 32:(pos + 1) * 32, :] = dot(w1v, fold[:, pos * 256:(pos + 1) * 256]).astype(BF16)
    w2s[...] = jnp.zeros(w2s.shape, F32)
    w2s[:, 0:864] = w2[...].astype(F32)
    planes = (1, 0, 2)
    for j in range(3):
        for slot, i in enumerate(planes):
            lane = i * 288 + j * 96
            w2c[j * 64:(j + 1) * 64, slot * 96:(slot + 1) * 96] = w2s[:, lane:lane + 96].astype(BF16)
    for t4 in range(7):
        turned = w2s[:, t4 * 128:(t4 + 1) * 128].T
        for quarter in range(4):
            t = t4 * 4 + quarter
            if t < 27:
                i, j, k = t // 9, (t // 3) % 3, t % 3
                block = turned[quarter * 32:(quarter + 1) * 32, :]
                wb[j * 96 + i * 32:j * 96 + (i + 1) * 32, k * 64:(k + 1) * 64] = block.astype(BF16)
    bias1 = column_of(b1[...])
    bias1 = jnp.concatenate([bias1] * 8, axis=0)
    bias2 = column_of(b2[...])
    c9[...] = jnp.zeros(c9.shape, BF16)
    cb[...] = jnp.zeros(cb.shape, BF16)
    gs[...] = jnp.zeros(gs.shape, BF16)
    part[448:512, :] = jnp.zeros((64, 128), BF16)

    r, s = iota((256, 256), 0), iota((256, 256), 1)
    rows = (r & 192) + (r & 3) * 16 + ((r >> 3) & 7) * 2 + ((r >> 2) & 1)
    move_rows = (rows == s).astype(F32)[0:128, 0:128].astype(BF16)
    move_lanes = (r == (s & 127) * 2 + (s >> 7)).astype(F32).astype(BF16)

    def lay_out(pair, b):
        flat = buf[pair * 2:pair * 2 + 2, b].reshape(128, 256)
        moved = dot(move_rows, dot(flat, move_lanes).astype(BF16)).reshape(2, 8, 8, 256)
        gap = jnp.zeros((2, 1, 8, 256), F32)
        low = jnp.concatenate([gap, moved[:, :7]], axis=1)
        high = jnp.concatenate([moved[:, 1:], gap], axis=1)
        odd = iota(moved.shape, 2) >= 4
        beside = jnp.where(odd, low, high)
        for xg, field in enumerate((moved, beside)):
            even_y, odd_y = field[..., :128], field[..., 128:]
            for yg in range(2):
                halves = (even_y, odd_y) if yg == 0 else (after(even_y), before(odd_y))
                tile = jnp.concatenate(halves, axis=2).astype(BF16)
                for z in range(2):
                    row = ((pair * 2 + z) * 4 + xg * 2 + yg) * 16
                    for x in range(8):
                        lane = (b * 8 + x) * 128
                        cols1[row:row + 16, lane:lane + 128] = tile[z, x]

    for b in range(2):
        lay_out(0, b)

    def fill(target, row, height, b, field, flip, cells=range(8)):
        for x in cells:
            lane = (b * 10 + 1 + x) * 128
            tile = field[:, x * 128:(x + 1) * 128].astype(F32)
            shifts = (before(tile), tile, after(tile))
            for k in range(3):
                piece = shifts[2 - k] if flip else shifts[k]
                target[row + k * height:row + (k + 1) * height, lane:lane + 128] = piece.astype(BF16)

    for b in range(2):
        wait_in(dens_copies[b])
        lay_out(1, b)
        for q in range(4):
            lane = b * 1024 + q * 256
            pre = dot(wbig[...], cols1[:, lane:lane + 256]) + bias1
            sig = sigmoid(pre)
            act = pre * sig
            d1[:, lane:lane + 256] = sig + act - act * sig
            total = act[0:32]
            for pos in range(1, 8):
                total = total + act[pos * 32:(pos + 1) * 32]
            pooled[b, :, q * 256:(q + 1) * 256] = (total * 0.125).astype(BF16)
            if q % 2 == 1:
                start(pool_copies[b * 2 + q // 2])
    for b in range(2):
        fill(c9, 0, 32, b, pooled[b].astype(F32), False)
        acc2[b] = dot(w2c[:, 0:96], c9[0:96, b * 1280:(b + 1) * 1280])
        trans[b] = cot[b].astype(F32)

    for b in range(2):
        for half in range(2):
            wait_in(pool_copies[b * 2 + half])
            for side in range(2):
                fill(c9, 96 + side * 96, 32, b, halo2.at[b, side], False, range(half * 4, half * 4 + 4))
        acc = acc2[b] + dot(w2c[:, 96:288], c9[96:288, b * 1280:(b + 1) * 1280])
        pre = acc[0:64, 0:1024] + acc[64:128, 128:1152] + acc[128:192, 256:1280] + bias2
        sig = sigmoid(pre)
        act = pre * sig
        slope = sig + act - act * sig
        grads = []
        for x in range(8):
            grads.append(trans[b, pl.ds(x, 64, stride=8), :] * slope[:, x * 128:(x + 1) * 128])
        grad = jnp.concatenate(grads, axis=1).astype(BF16)
        for j in range(3):
            lane = b * 1280 + j * 128
            gs[j * 64:(j + 1) * 64, lane:lane + 1024] = grad
        grad = grad.astype(F32)
        fill(cb, 0, 64, b, grad, True)
        acc = dot(wb[...], cb[:, b * 1280:(b + 1) * 1280])
        give = acc[0:96, 256:1280] + acc[96:192, 128:1152] + acc[192:288, 0:1024]
        bsend[b, 1] = give[0:32].astype(BF16)
        bsend[b, 0] = give[64:96].astype(BF16)
        start(back_copies[b])
        bown[:, b * 1024:(b + 1) * 1024] = give[32:64]
        acts[b] = act

    total = dot_nt(gs[...], c9[...])
    for j in range(3):
        for slot, i in enumerate(planes):
            lane = i * 288 + j * 96
            w2s[:, lane:lane + 96] = total[j * 64:(j + 1) * 64, slot * 96:(slot + 1) * 96]
    for t in range(7):
        part[t * 64:(t + 1) * 64, :] = w2s[:, t * 128:(t + 1) * 128].astype(BF16)

    size = 512 // ns

    def chunk(index):
        return pl.ds(pl.multiple_of(index * size, size), size)

    def rs_copy(d):
        return remote(part.at[chunk(lax.rem(si + d, ns))], rs_recv.at[d], rsend.at[d], rrecv.at[d], space_peer(d))

    def bx_copy(d):
        return remote(mine.at[0], bx_recv.at[bi], xsend.at[d], xrecv.at[d], batch_peer(d))

    def ag_copy(d):
        return remote(mine.at[1], full.at[chunk(si)], gsend.at[d], grecv.at[d], space_peer(d))

    def s1_copy(d):
        return remote(small, sm_recv.at[si], s1send.at[d], s1recv.at[d], space_peer(d))

    def s2_copy(d):
        return remote(sm_mid, sm_recv2.at[bi], s2send.at[d], s2recv.at[d], batch_peer(d))

    def each(count, make, act):
        every(range(1, count), lambda d: act(make(d)))

    def go(copy):
        copy.start()

    def arrive(copy):
        copy.wait_recv()

    def leave(copy):
        copy.wait_send()

    def in_order(terms, count):
        total = terms[0].astype(F32)
        for index in range(1, count):
            total = total + terms[index].astype(F32)
        return total

    live = -(-448 // size)

    def rs_go(d):
        pl.when(lax.rem(si + d, ns) < live)(rs_copy(d).start)

    def rs_leave(d):
        pl.when(lax.rem(si + d, ns) < live)(rs_copy(d).wait_send)

    def ag_arrive(d):
        pl.when(lax.rem(si + ns - d, ns) < live)(ag_copy(d).wait_recv)

    every(range(1, ns), rs_go)

    gb2 = jnp.sum(gs[64:128, :].astype(F32), axis=1, keepdims=True)
    for b in range(2):
        for x in range(8):
            trans[b, pl.ds(x, 64, stride=8), :] = acts[b, :, x * 128:(x + 1) * 128]
        feat[b] = trans[b].astype(BF16)

    gb1 = jnp.zeros((32, 256), F32)
    for b in range(2):
        wait_in(back_copies[b])
        for q in range(4):
            lane = b * 1024 + q * 256
            near = brecv[b, :, :, q * 256:(q + 1) * 256].astype(F32)
            back = (bown[:, lane:lane + 256] + near[0] + near[1]) * 0.125
            for pos in range(8):
                piece = (back * d1[pos * 32:(pos + 1) * 32, lane:lane + 256]).astype(BF16)
                gf[pos * 32:(pos + 1) * 32, lane:lane + 256] = piece
                gb1 = gb1 + piece.astype(F32)
        term = dot_nt(gf[:, b * 1024:(b + 1) * 1024], cols1[:, b * 1024:(b + 1) * 1024])
        if b == 0:
            held[...] = term
    gram = held[...] + term
    high = gram.astype(BF16)
    low = (gram - high.astype(F32)).astype(BF16)
    both = jnp.concatenate([
        jnp.concatenate([term[pos * 32:(pos + 1) * 32] for pos in range(8)], axis=1) for term in (high, low)
    ], axis=0)
    folded = dot_nt(both, fold[...])
    lane = iota((32, 128), 1)
    sums = folded[0:32] + folded[32:64]
    sums = jnp.where(lane == 108, jnp.sum(gb1, axis=1, keepdims=True), sums)
    sums = jnp.where(lane == 109, gb2[0:32], sums)
    small[...] = jnp.where(lane == 110, gb2[32:64], sums).astype(BF16)
    each(ns, s1_copy, go)

    @pl.when(si < live)
    def space_sum():
        each(ns, rs_copy, arrive)
        total = part[chunk(si), :].astype(F32)
        for d in range(1, ns):
            total = total + rs_recv[d].astype(F32)
        total = total.astype(BF16)
        mine[0] = total
        bx_recv[bi] = total
        each(nb, bx_copy, go)

    each(ns, s1_copy, arrive)
    sm_recv[si] = small[...]
    total = in_order(sm_recv, ns).astype(BF16)
    sm_mid[...] = total
    sm_recv2[bi] = total
    each(nb, s2_copy, go)

    @pl.when(si < live)
    def batch_sum():
        each(nb, bx_copy, arrive)
        total = in_order(bx_recv, nb).astype(BF16)
        mine[1] = total
        full[chunk(si), :] = total
        each(ns, ag_copy, go)

    for b in range(2):
        wait_out(dens_copies[b])
        wait_out(pool_copies[b * 2])
        wait_out(pool_copies[b * 2 + 1])
        wait_out(back_copies[b])
    every(range(1, ns), rs_leave)
    each(ns, s1_copy, leave)
    each(nb, s2_copy, arrive)
    total = in_order(sm_recv2, nb)
    gw1_out[...] = total[:, 0:108]
    gb1_out[...] = row_of(total[:, 108:109])
    gb2_out[...] = row_of(jnp.concatenate([total[:, 109:110], total[:, 110:111]], axis=0))

    each(nb, s2_copy, leave)
    every(range(1, ns), ag_arrive)
    for t in range(7):
        width = min(128, 864 - t * 128)
        gw2_out[:, t * 128:t * 128 + width] = full[t * 64:(t + 1) * 64, 0:width].astype(F32)

    @pl.when(si < live)
    def done():
        each(nb, bx_copy, leave)
        each(ns, ag_copy, leave)


def hand_out(*refs):
    held, results, sems = refs[0:5], refs[5:10], refs[10]
    outward = [pltpu.make_async_copy(held[n], results[n], sems.at[n]) for n in range(5)]
    for copy in outward:
        copy.start()
    for copy in outward:
        copy.wait()


def body(nb, ns, density, w_first, b_first, w_second, b_second, cotangent):
    vmem = pl.BlockSpec(memory_space=pltpu.VMEM)
    hbm = pl.BlockSpec(memory_space=pltpu.HBM)
    dma = pltpu.SemaphoreType.DMA
    size = 512 // ns
    shapes = (
        jax.ShapeDtypeStruct((2, 512, 128), BF16),
        jax.ShapeDtypeStruct((32, 108), F32),
        jax.ShapeDtypeStruct((1, 32), F32),
        jax.ShapeDtypeStruct((64, 864), F32),
        jax.ShapeDtypeStruct((1, 64), F32),
    )
    held = pl.pallas_call(
        functools.partial(kernel, nb, ns),
        out_shape=tuple(pltpu.VMEM(one.shape, one.dtype) for one in shapes),
        in_specs=[hbm] * 7,
        out_specs=(vmem,) * 5,
        scratch_shapes=[
            pltpu.VMEM((32, 108), BF16),
            pltpu.VMEM((1, 32), F32),
            pltpu.VMEM((64, 864), BF16),
            pltpu.VMEM((1, 64), F32),
            pltpu.VMEM((2, 512, 128), BF16),
            pltpu.VMEM((128, 2048), BF16),
            pltpu.VMEM((4, 2, 4, 16, 256), BF16),
            pltpu.VMEM((256, 2048), BF16),
            pltpu.VMEM((256, 256), BF16),
            pltpu.VMEM((256, 2048), F32),
            pltpu.VMEM((32, 128), F32),
            pltpu.VMEM((64, 896), F32),
            pltpu.VMEM((192, 288), BF16),
            pltpu.VMEM((288, 192), BF16),
            pltpu.VMEM((2, 32, 1024), BF16),
            pltpu.VMEM((2, 2, 32, 1024), BF16),
            pltpu.VMEM((288, 2560), BF16),
            pltpu.VMEM((2, 192, 1280), F32),
            pltpu.VMEM((2, 512, 128), F32),
            pltpu.VMEM((2, 64, 1024), F32),
            pltpu.VMEM((256, 256), F32),
            pltpu.VMEM((192, 2560), BF16),
            pltpu.VMEM((192, 2560), BF16),
            pltpu.VMEM((2, 2, 32, 1024), BF16),
            pltpu.VMEM((2, 2, 32, 1024), BF16),
            pltpu.VMEM((32, 2048), F32),
            pltpu.VMEM((256, 2048), BF16),
            pltpu.VMEM((512, 128), BF16),
            pltpu.VMEM((ns, size, 128), BF16),
            pltpu.VMEM((2, size, 128), BF16),
            pltpu.VMEM((nb, size, 128), BF16),
            pltpu.VMEM((512, 128), BF16),
            pltpu.VMEM((32, 128), BF16),
            pltpu.VMEM((ns, 32, 128), BF16),
            pltpu.VMEM((32, 128), BF16),
            pltpu.VMEM((nb, 32, 128), BF16),
            dma((2,)), dma((6,)), dma((2, 2)), dma((2, 2)),
            dma((4, 2)), dma((4, 2)), dma((2, 2)), dma((2, 2)),
            dma((ns,)), dma((ns,)), dma((nb,)), dma((nb,)), dma((ns,)), dma((ns,)),
            dma((ns,)), dma((ns,)), dma((nb,)), dma((nb,)),
        ],
        compiler_params=pltpu.CompilerParams(
            collective_id=0, has_side_effects=True, vmem_limit_bytes=40 * 1024 * 1024
        ),
        cost_estimate=pl.CostEstimate(flops=1 << 30, bytes_accessed=1 << 21, transcendentals=1 << 20),
    )(*[
        pltpu.with_memory_space_constraint(one, pltpu.HBM)
        for one in (
            density, w_first, b_first.reshape(1, 32), w_second, b_second.reshape(1, 64), cotangent.reshape(2, 512, 128),
            jnp.asarray(fold_matrix(), BF16),
        )
    ])
    feat, gw1, gb1, gw2, gb2 = pl.pallas_call(
        hand_out,
        out_shape=shapes,
        in_specs=[vmem] * 5,
        out_specs=(hbm,) * 5,
        scratch_shapes=[dma((5,))],
        compiler_params=pltpu.CompilerParams(vmem_limit_bytes=8 * 1024 * 1024),
    )(*held)
    return feat.reshape(cotangent.shape), gw1, gb1.reshape(32), gw2, gb2.reshape(64)


def solution(mesh):
    data = P("batch", None, "space", None, None)
    return jax.shard_map(
        functools.partial(body, mesh.shape["batch"], mesh.shape["space"]),
        mesh=mesh,
        in_specs=(data, P(), P(), P(), P(), data),
        out_specs=(data, P(), P(), P(), P()),
        check_vma=False,
    )
```
